256 devices in a mesh: dp: 16 (over z, core), cent: 16 (over x, y).
Axes of the slice: x: 4, y: 4, z: 8, core: 2. Of those that a mesh axis runs over, the one named last changes fastest.
Arguments:
- points: bfloat16 [262144, 1152], P(('dp', 'cent')), may hold values from -150 to 150
- candidates: int32 [1024, 8], P(('dp', 'cent')), may hold values from 0 to 127, as said below
- centroids: bfloat16 [128, 256, 1152], P('cent'), may hold values from -6 to 6
Outputs:
- new_centroids: float32 [128, 256, 1152], P('cent', 'dp')
- masses: float32 [128, 256], P('cent', 'dp')
The draws below stay inside these ranges and needn't reach their ends.
Inputs may be any that keep to these rules, and one draw needn't show every extreme that they name: `candidates`: each row names 8 different blocks. The 4 rows of one aligned group together name exactly 16 different blocks, exactly 1 of them in each run of 8 consecutive blocks starting at a multiple of 8. Every block is named by some row.
All inputs are finite; a program needn't handle non-finite values.
Results may differ from the reference program's by a relative error of at most 0.0016.
Values may be sent and summed in bfloat16 or wider, within the bound.
No kernel may reach another device: no remote copies, remote signals or barrier semaphores. Data moves between devices by JAX's collectives and lax.ppermute only.
A program may use at most 128 MiB of HBM per device.

```python
import jax
import jax.numpy as jnp
from jax import lax

D = 1152
BS = 256
CAND = 8
FETCH = 16
PB_DEV = 4
CB_OWN = 8
PBLOCKS = 1024
POINTS = 262144
BLOCKS = 128


def shared_centroids(key):
    subkey = jax.random.fold_in(key, 101)
    return jnp.clip(jax.random.normal(subkey, (BLOCKS, BS, D), jnp.float32), -6.0, 6.0)


def shared_candidates(key):
    subkey = jax.random.fold_in(key, 202)
    perm_key, order_key, jitter_key = jax.random.split(subkey, 3)
    groups = PBLOCKS // PB_DEV
    owners = BLOCKS // CB_OWN
    per_owner = FETCH // owners
    owner_perms = jax.vmap(lambda sub_key: jax.random.permutation(sub_key, groups))(jax.random.split(perm_key, owners))
    start_at = owner_perms.T % CB_OWN
    step_range = jnp.arange(per_owner, dtype=jnp.int32)
    local_ids = (start_at[:, :, None] + step_range[None, None, :]) % CB_OWN
    fetched = (jnp.arange(owners, dtype=jnp.int32)[None, :, None] * CB_OWN + local_ids).reshape(groups, FETCH)
    slot_order = jax.vmap(lambda sub_key: jax.random.permutation(sub_key, FETCH))(jax.random.split(order_key, groups))
    shuffled = jnp.take_along_axis(fetched, slot_order, axis=1)
    window_min = -(-FETCH // PB_DEV)
    jitter_top = min(CAND - window_min, FETCH // PB_DEV)
    base_offset = jnp.arange(PB_DEV, dtype=jnp.int32) * FETCH // PB_DEV
    jitter = jax.random.randint(jitter_key, (groups, PB_DEV), 0, jitter_top + 1)
    jitter = jitter * (jnp.arange(PB_DEV) > 0).astype(jnp.int32)[None, :]
    offsets = base_offset[None, :] + jitter
    positions = (offsets[:, :, None] + jnp.arange(CAND, dtype=jnp.int32)[None, None, :]) % FETCH
    picked = shuffled[jnp.arange(groups)[:, None, None], positions]
    return picked.reshape(PBLOCKS, CAND).astype(jnp.int32)


def draw_centroids(key, part):
    return shared_centroids(key).astype(jnp.bfloat16)


def draw_candidates(key, part):
    return shared_candidates(key)


def draw_points(key, part):
    key = jax.random.fold_in(key, 3)
    values = jnp.clip(jax.random.normal(key, (POINTS, D), jnp.float32), -6.0, 6.0)
    return values.astype(jnp.bfloat16)


def setup_inputs(seed: int = 0) -> dict:
    key_of = jax.random.split(jax.random.key(seed), 4)
    points = draw_points(jax.random.fold_in(key_of[3], 71), 0)
    candidates = draw_candidates(jax.random.fold_in(key_of[3], 71), 0)
    centroids = draw_centroids(jax.random.fold_in(key_of[3], 71), 0)
    return dict(points=points, candidates=candidates, centroids=centroids)


inverse_temp = 0.03125


def reference(points, candidates, centroids):
    groups = PBLOCKS // PB_DEV
    norms_all = jnp.sum(jnp.square(centroids.astype(jnp.float32)), axis=-1)

    def device_terms(group_id):
        id_rows = lax.dynamic_slice_in_dim(candidates, (group_id * PB_DEV).astype(jnp.int32), PB_DEV, 0)
        point_rows = lax.dynamic_slice_in_dim(points, (group_id * (PB_DEV * BS)).astype(jnp.int32), PB_DEV * BS, 0)
        point_rows = point_rows.reshape(PB_DEV, BS, D)
        pieces = []
        masses_list = []
        for position in range(PB_DEV):
            picked = jnp.take(centroids, id_rows[position], axis=0).reshape(CAND * BS, D)
            picked_norms = jnp.take(norms_all, id_rows[position], axis=0).reshape(-1)
            scores = (jnp.dot(point_rows[position], picked.T, preferred_element_type=jnp.float32) - 0.5 * picked_norms[None, :]) * inverse_temp
            highest = jnp.max(scores, axis=1, keepdims=True)
            lifted = jnp.exp(scores - highest)
            shares = lifted / jnp.sum(lifted, axis=1, keepdims=True)
            weights = shares.astype(jnp.bfloat16)
            pieces.append(jnp.dot(weights.T, point_rows[position], preferred_element_type=jnp.float32).reshape(CAND, BS, D))
            masses_list.append(jnp.sum(shares, axis=0).reshape(CAND, BS))
        stacked = jnp.concatenate(pieces, axis=0)
        mass_stack = jnp.concatenate(masses_list, axis=0)
        flat_ids = id_rows.reshape(-1)
        same_ids = (flat_ids[:, None] == flat_ids[None, :]).astype(jnp.float32)
        merged = jnp.einsum("kj,jbd->kbd", same_ids, stacked, precision=lax.Precision.HIGHEST)
        merged_mass = jnp.einsum("kj,jb->kb", same_ids, mass_stack, precision=lax.Precision.HIGHEST)
        earlier = jnp.sum(jnp.tril(same_ids, -1), axis=1)
        leading = (earlier == 0.0).astype(jnp.float32)
        rounded = lax.optimization_barrier(merged.astype(jnp.bfloat16)).astype(jnp.float32) * leading[:, None, None]
        mass_rounded = lax.optimization_barrier(merged_mass.astype(jnp.bfloat16)).astype(jnp.float32) * leading[:, None]
        return flat_ids, rounded, mass_rounded

    def add_device(running, group_id):
        totals, total_mass = running
        flat_ids, rounded, mass_rounded = device_terms(group_id)
        return (totals.at[flat_ids].add(rounded), total_mass.at[flat_ids].add(mass_rounded)), None

    start_state = (jnp.zeros((BLOCKS, BS, D), jnp.float32), jnp.zeros((BLOCKS, BS), jnp.float32))
    final_state, _ = lax.scan(add_device, start_state, jnp.arange(groups, dtype=jnp.int32))
    totals, total_mass = final_state
    new_centroids = (totals + centroids.astype(jnp.float32)) / (total_mass + 1.0)[:, :, None]
    return new_centroids, total_mass
```

```python
import functools

import jax
import jax.numpy as jnp
from jax import lax
from jax.experimental import pallas as pl
from jax.experimental.pallas import tpu as pltpu
from jax.sharding import PartitionSpec as P

SIDE = 4
PAIRS = SIDE * SIDE
inverse_temp = 0.03125
LOW = -1e30
VMEM = 56 * 1024 * 1024
BID, MASK, CORE = 0, PAIRS, PAIRS + 4 * PAIRS
NEAR = [(r, s) for r in (0, 1, 3) for s in (0, 1, 3)]
FAR = [(r, 2) for r in (0, 1, 3)] + [(2, s) for s in (0, 1, 3, 2)]
AWAY = (
    [(r, 1) for r in range(4)]
    + [(0, 2), (1, 2)]
    + [(r, 3) for r in range(4)]
    + [(2, 2), (3, 2)]
)
HERE = [(r, 0) for r in range(4)]
SPLIT = 512


def score_kernel(x_groups, c_owners, carry, tab, seq, *refs):
    refs = list(refs)
    x_refs = {r: [refs.pop(0) for _ in range(n)] for r, n in x_groups}
    c_refs = {s: [refs.pop(0) for _ in range(n)] for s, n in c_owners}
    if carry:
        _, m_in, l_in = refs[:3]
        refs = refs[3:]
    score_ref, m_ref, l_ref, xbuf, cbuf, xsem, csem = refs
    step = pl.program_id(0)
    last = pl.num_programs(0) - 1
    block = cbuf.shape[1]

    def start_c(at):
        r, owner = seq[5 * at], seq[5 * at + 1]
        slot = lax.rem(at, 2)
        bid = tab[BID + SIDE * r + owner]
        other = jnp.where(bid // 4 == tab[CORE], 0, 1)
        for s, parts in c_refs.items():
            each = parts[0].shape[0]
            which = other * (4 // each) + lax.rem(bid, 4) // each if len(parts) > 1 else 0
            for q, part in enumerate(parts):

                @pl.when((owner == s) & (which == q))
                def _():
                    pltpu.make_async_copy(
                        part.at[lax.rem(bid, each)], cbuf.at[slot], csem.at[slot]
                    ).start()

    def start_x(group, slot):
        for r, parts in x_refs.items():
            tall = parts[0].shape[0]

            @pl.when(group == r)
            def _():
                for h, part in enumerate(parts):
                    pltpu.make_async_copy(
                        part, xbuf.at[slot, pl.ds(h * tall, tall)], xsem.at[slot]
                    ).start()

    group, owner, first, xslot, following = [seq[5 * step + i] for i in range(5)]
    cslot = lax.rem(step, 2)

    @pl.when(step == 0)
    def _():
        start_x(group, xslot)
        start_c(0)

    @pl.when(step < last)
    def _():
        start_c(step + 1)

    @pl.when(first == 1)
    def _():
        start_x(following, 1 - xslot)
        pltpu.make_async_copy(xbuf.at[xslot], xbuf.at[xslot], xsem.at[xslot]).wait()
        if carry:
            fresh = group == 2
            m_ref[...] = jnp.where(fresh, LOW, m_in[...])
            l_ref[...] = jnp.where(fresh, 0.0, l_in[...])
        else:
            m_ref[...] = jnp.full(m_ref.shape, LOW, jnp.float32)
            l_ref[...] = jnp.zeros(l_ref.shape, jnp.float32)

    pltpu.make_async_copy(cbuf.at[cslot], cbuf.at[cslot], csem.at[cslot]).wait()
    wide = cbuf[cslot].astype(jnp.float32)
    half_norm = 0.5 * jnp.sum(wide * wide, axis=1, keepdims=True)
    for p in range(4):

        @pl.when(tab[MASK + 4 * (SIDE * group + owner) + p] == 1)
        def _():
            x = xbuf[xslot, pl.ds(p * block, block), :]
            dots = lax.dot_general(
                cbuf[cslot], x, (((1,), (1,)), ((), ())), preferred_element_type=jnp.float32
            )
            scores = (dots - half_norm) * inverse_temp
            score_ref[0, p] = scores
            old = m_ref[0, p : p + 1, :]
            new = jnp.maximum(old, jnp.max(scores, axis=0, keepdims=True))
            m_ref[0, p : p + 1, :] = new
            l_ref[0, p : p + 1, :] = l_ref[0, p : p + 1, :] * jnp.exp(old - new) + jnp.sum(
                jnp.exp(scores - new), axis=0, keepdims=True
            )


def score_call(tab, pairs, xs, cs, rows, carried=None):
    features = cs[0][0].shape[2]
    block = cs[0][0].shape[1]
    visits = []
    for r, _ in pairs:
        if r not in visits:
            visits.append(r)
    seq, seen = [], set()
    for r, s in pairs:
        at = visits.index(r)
        following = visits[at + 1] if at + 1 < len(visits) else -1
        seq += [r, s, int(r not in seen), at % 2, following]
        seen.add(r)
    seq = jnp.array(seq, jnp.int32)
    stat = jax.ShapeDtypeStruct((SIDE, 4, block), jnp.float32)
    stat_spec = pl.BlockSpec((1, 4, block), lambda i, tab, seq: (seq[5 * i], 0, 0))
    x_groups = tuple((r, len(parts)) for r, parts in xs.items())
    c_owners = tuple((s, len(parts)) for s, parts in cs.items())
    operands = [v for parts in xs.values() for v in parts]
    operands += [v for parts in cs.values() for v in parts]
    in_specs = [pl.BlockSpec(memory_space=pl.ANY)] * len(operands)
    aliases = {}
    if carried is not None:
        aliases = {2 + len(operands): 0}
        operands += list(carried)
        in_specs += [pl.BlockSpec(memory_space=pl.ANY), stat_spec, stat_spec]
    return pl.pallas_call(
        functools.partial(score_kernel, x_groups, c_owners, carried is not None),
        grid_spec=pltpu.PrefetchScalarGridSpec(
            num_scalar_prefetch=2,
            grid=(len(pairs),),
            in_specs=in_specs,
            out_specs=[
                pl.BlockSpec(
                    (1, 4, block, block),
                    lambda i, tab, seq: (SIDE * seq[5 * i] + seq[5 * i + 1], 0, 0, 0),
                ),
                stat_spec,
                stat_spec,
            ],
            scratch_shapes=[
                pltpu.VMEM((2, rows, features), jnp.bfloat16),
                pltpu.VMEM((2, block, features), jnp.bfloat16),
                pltpu.SemaphoreType.DMA((2,)),
                pltpu.SemaphoreType.DMA((2,)),
            ],
        ),
        out_shape=[jax.ShapeDtypeStruct((PAIRS, 4, block, block), jnp.float32), stat, stat],
        input_output_aliases=aliases,
        compiler_params=pltpu.CompilerParams(vmem_limit_bytes=VMEM),
        cost_estimate=pl.CostEstimate(
            flops=4 * len(pairs) * block * block * features,
            bytes_accessed=2_200_000 * len(pairs),
            transcendentals=2 * len(pairs) * block * block,
        ),
        name="scores",
    )(tab, seq, *operands)


def sum_kernel(x_groups, counts, tab, seq, *refs):
    refs = list(refs)
    x_refs = {r: [refs.pop(0) for _ in range(n)] for r, n in x_groups}
    score_ref, m_ref, r_ref = refs[:3]
    outs = refs[3 : 3 + 2 * len(counts)]
    xbuf, acc, macc, sem = refs[3 + 2 * len(counts) :]
    step = pl.program_id(0)
    rows = xbuf.shape[0] // SIDE
    block = acc.shape[0]

    @pl.when(step == 0)
    def _():
        for r, parts in x_refs.items():
            tall = parts[0].shape[0]
            for h, part in enumerate(parts):
                pltpu.make_async_copy(
                    part, xbuf.at[pl.ds(r * rows + h * tall, tall)], sem.at[r]
                ).start()

    @pl.when(step < SIDE)
    def _():
        here = xbuf.at[pl.ds(0, rows)]
        pltpu.make_async_copy(here, here, sem.at[step]).wait()

    pair = seq[step]
    group = pair // SIDE
    acc[...] = jnp.zeros(acc.shape, jnp.float32)
    macc[...] = jnp.zeros(macc.shape, jnp.float32)
    for p in range(4):

        @pl.when(tab[MASK + 4 * pair + p] == 1)
        def _():
            shares = jnp.exp(score_ref[0, p] - m_ref[group, p : p + 1, :]) * r_ref[
                group, p : p + 1, :
            ]
            x = xbuf[pl.ds(pl.multiple_of(group * rows, rows) + p * block, block), :]
            acc[...] += lax.dot_general(
                shares.astype(jnp.bfloat16),
                x,
                (((1,), (0,)), ((), ())),
                preferred_element_type=jnp.float32,
            )
            macc[...] += shares[:, :128] + shares[:, 128:]

    def write(left, right):
        left[0, 0:block, :] = acc[:, :SPLIT].astype(jnp.bfloat16)
        right[0] = acc[:, SPLIT:].astype(jnp.bfloat16)
        mass = jnp.sum(jnp.transpose(macc[...]), axis=0, keepdims=True)
        left[0, block:, 0:block] = jnp.broadcast_to(mass, (16, block)).astype(jnp.bfloat16)
        left[0, block:, block:] = jnp.zeros((16, SPLIT - block), jnp.bfloat16)

    begin = 0
    for i, n in enumerate(counts):

        @pl.when((step >= begin) & (step < begin + n))
        def _():
            write(outs[2 * i], outs[2 * i + 1])

        begin += n


def sum_call(tab, pairs, counts, xs, rows, scores, top, inverse):
    block = scores.shape[-1]
    features = xs[0][0].shape[1]
    out_specs, out_shape = [], []
    begin = 0
    for n in counts:
        for tall, width in ((block + 16, SPLIT), (block, features - SPLIT)):
            out_specs.append(
                pl.BlockSpec(
                    (1, tall, width),
                    lambda i, tab, seq, b=begin, n=n: (jnp.clip(i - b, 0, n - 1), 0, 0),
                )
            )
            out_shape.append(jax.ShapeDtypeStruct((n, tall, width), jnp.bfloat16))
        begin += n
    seq = jnp.array([SIDE * r + s for r, s in pairs], jnp.int32)
    whole = pl.BlockSpec((SIDE, 4, block), lambda i, tab, seq: (0, 0, 0))
    operands = [v for parts in xs.values() for v in parts]
    x_groups = tuple((r, len(parts)) for r, parts in xs.items())
    return pl.pallas_call(
        functools.partial(sum_kernel, x_groups, counts),
        grid_spec=pltpu.PrefetchScalarGridSpec(
            num_scalar_prefetch=2,
            grid=(len(pairs),),
            in_specs=[pl.BlockSpec(memory_space=pl.ANY)] * len(operands)
            + [
                pl.BlockSpec((1, 4, block, block), lambda i, tab, seq: (seq[i], 0, 0, 0)),
                whole,
                whole,
            ],
            out_specs=out_specs,
            scratch_shapes=[
                pltpu.VMEM((SIDE * rows, features), jnp.bfloat16),
                pltpu.VMEM((block, features), jnp.float32),
                pltpu.VMEM((block, 128), jnp.float32),
                pltpu.SemaphoreType.DMA((SIDE,)),
            ],
        ),
        out_shape=out_shape,
        compiler_params=pltpu.CompilerParams(vmem_limit_bytes=VMEM),
        cost_estimate=pl.CostEstimate(
            flops=4 * len(pairs) * block * block * features,
            bytes_accessed=9_500_000 + 1_700_000 * len(pairs),
            transcendentals=2 * len(pairs) * block * block,
        ),
        name="sums",
    )(tab, seq, *operands, scores, top, inverse)


def entries_of(here, up, down, far_up, far_down):
    return (
        [(here, i) for i in range(4)]
        + [(up, i) for i in range(4)]
        + [(down, i) for i in range(4)]
        + [(far_up, i) for i in range(2)]
        + [(far_down, i) for i in range(2)]
    )


def merge_kernel(ids, here, up, down, far_up, far_down, out):
    out[...] = jnp.zeros(out.shape, jnp.float32)
    for e, (ref, i) in enumerate(entries_of(here, up, down, far_up, far_down)):
        out[0, ids[e]] += ref[i].astype(jnp.float32)


def merge_call(ids, arrays, side, own_blocks, block):
    width = arrays[0].shape[-1]
    parts = block // 32
    table = jnp.concatenate([ids, side.reshape(1)])

    def spec(n):
        return pl.BlockSpec((n, 16, width), lambda i, ids: (0, 2 * i + ids[PAIRS], 0))

    return pl.pallas_call(
        merge_kernel,
        grid_spec=pltpu.PrefetchScalarGridSpec(
            num_scalar_prefetch=1,
            grid=(parts,),
            in_specs=[spec(4), spec(4), spec(4), spec(2), spec(2)],
            out_specs=pl.BlockSpec((1, own_blocks, 16, width), lambda i, ids: (i, 0, 0, 0)),
        ),
        out_shape=jax.ShapeDtypeStruct((parts, own_blocks, 16, width), jnp.float32),
        compiler_params=pltpu.CompilerParams(vmem_limit_bytes=VMEM),
        cost_estimate=pl.CostEstimate(
            flops=8 * block * width, bytes_accessed=16 * block * width, transcendentals=0
        ),
        name="merge",
    )(table, *arrays)


def mass_kernel(ids, here, up, down, far_up, far_down, out):
    out[...] = jnp.zeros(out.shape, jnp.float32)
    for e, (ref, i) in enumerate(entries_of(here, up, down, far_up, far_down)):
        row = ref[i][:, : out.shape[-1]].astype(jnp.float32)
        out[ids[e]] += row[0:8, :]


def mass_call(ids, arrays, own_blocks, block):
    width = arrays[0].shape[-1]

    def spec(n):
        return pl.BlockSpec((n, 16, width), lambda i, ids: (0, block // 16, 0))

    return pl.pallas_call(
        mass_kernel,
        grid_spec=pltpu.PrefetchScalarGridSpec(
            num_scalar_prefetch=1,
            grid=(1,),
            in_specs=[spec(4), spec(4), spec(4), spec(2), spec(2)],
            out_specs=pl.BlockSpec((own_blocks, 8, block), lambda i, ids: (0, 0, 0)),
        ),
        out_shape=jax.ShapeDtypeStruct((own_blocks, 8, block), jnp.float32),
        name="masses",
    )(ids, *arrays)


def shift_x(value, by):
    pairs = [
        (SIDE * x + y, SIDE * ((x + by) % SIDE) + y) for x in range(SIDE) for y in range(SIDE)
    ]
    return lax.ppermute(value, "cent", pairs)


def shift_y(value, by):
    pairs = [
        (SIDE * x + y, SIDE * x + (y + by) % SIDE) for x in range(SIDE) for y in range(SIDE)
    ]
    return lax.ppermute(value, "cent", pairs)


def swap_core(value):
    return lax.ppermute(value, "dp", [(i, i ^ 1) for i in range(16)])


def tables(candidates, own_blocks):
    place = lax.axis_index("cent")
    x, y = place // SIDE, place % SIDE
    core = (lax.axis_index("dp") % 2).astype(jnp.int32)
    every = jnp.stack([candidates] + [shift_x(candidates, -r) for r in (1, 2, 3)])
    owner, local = every // own_blocks, every % own_blocks
    line = SIDE * x + (y + jnp.arange(SIDE, dtype=jnp.int32)) % SIDE
    named = owner[:, None] == line[None, :, None, None]
    bid = jnp.max(jnp.where(named, local[:, None], 0), axis=(2, 3)).astype(jnp.int32)
    mask = jnp.any(named, axis=3).astype(jnp.int32)
    tab = jnp.concatenate([bid.reshape(-1), mask.reshape(-1), core.reshape(1)])
    ids = jnp.concatenate(
        [bid[:, 0], shift_y(bid[:, 1], 1), shift_y(bid[:, 3], -1), shift_y(bid[:, 2], 2)]
    )
    return tab, ids, core


def per_device(points, candidates, centroids):
    own_blocks, block, features = centroids.shape
    rows = points.shape[0]
    stripe = lax.axis_size("dp")
    rows_each = block // stripe
    dp_place = lax.axis_index("dp")
    tab, ids, core = tables(candidates, own_blocks)

    half = rows // 2
    share = own_blocks // 2
    mine = lax.dynamic_slice_in_dim(centroids, core * share, share, 0)
    x3, x1 = shift_x(points, 1), shift_x(points, -1)
    c3, c1 = shift_y(mine, 1), shift_y(mine, -1)
    x2a, x2b = shift_x(x3[:half], 1), shift_x(x1[half:], -1)
    c2a, c2b = shift_y(c3[: share // 2], 1), shift_y(c1[share // 2 :], -1)
    xs = {0: [points], 1: [x1], 3: [x3]}
    cs = {0: [centroids], 1: [c1, swap_core(c1)], 3: [c3, swap_core(c3)]}
    near = score_call(tab, NEAR, xs, cs, rows)
    xs[2] = [x2a, x2b]
    cs[2] = [c2a, c2b, swap_core(c2a), swap_core(c2b)]
    scores, top, total = score_call(tab, FAR, xs, cs, rows, near)

    stats = jnp.stack([top, total])
    tops, totals = [top], [total]
    for by in (1, 2, 3):
        moved = jnp.roll(shift_x(stats, -by), by, axis=1)
        tops.append(moved[0])
        totals.append(moved[1])
    highest = functools.reduce(jnp.maximum, tops)
    whole = sum(t * jnp.exp(m - highest) for m, t in zip(tops, totals))
    inverse = 1.0 / whole

    sums = sum_call(tab, AWAY, (6, 6), xs, rows, scores, highest, inverse)
    here = sum_call(tab, HERE, (4,), xs, rows, scores, highest, inverse)
    previous = lax.dynamic_slice_in_dim(centroids, dp_place * rows_each, rows_each, 1).astype(
        jnp.float32
    )
    lines = [[2 * z + c for z in range(stripe // 2)] for c in range(2)]
    out = []
    for k in range(2):
        up, down = sums[k], sums[2 + k]
        from_up, from_down = shift_y(up, 1), shift_y(down, -1)
        far_up, far_down = shift_y(from_up[4:], 1), shift_y(from_down[4:], -1)
        arrays = (here[k], from_up, from_down, far_up, far_down)
        if k == 0:
            mass = mass_call(ids, arrays, own_blocks, block)[:, 0, :]
            mass = mass.reshape(own_blocks, stripe, rows_each).transpose(1, 0, 2)
            mass = lax.all_to_all(mass, "dp", split_axis=0, concat_axis=0, tiled=True)
            new_mass = jnp.sum(mass, axis=0)
        other = swap_core(merge_call(ids, arrays, 1 - core, own_blocks, block))
        both = merge_call(ids, arrays, core, own_blocks, block) + other
        new_sums = lax.psum_scatter(
            both, "dp", scatter_dimension=0, axis_index_groups=lines, tiled=True
        )[0]
        part = previous[:, :, :SPLIT] if k == 0 else previous[:, :, SPLIT:]
        out.append((new_sums + part) / (new_mass + 1.0)[:, :, None])
    return jnp.concatenate(out, axis=2), new_mass


def solution(mesh):
    in_specs = (P(("dp", "cent"), None), P(("dp", "cent"), None), P("cent", None, None))
    out_specs = (P("cent", "dp", None), P("cent", "dp"))
    return jax.shard_map(
        per_device, mesh=mesh, in_specs=in_specs, out_specs=out_specs, check_vma=False
    )
```

```python
import functools

import jax
import jax.numpy as jnp
from jax import lax
from jax.experimental import pallas as pl
from jax.experimental.pallas import tpu as pltpu
from jax.sharding import PartitionSpec as P

SIDE = 4
PAIRS = SIDE * SIDE
inverse_temp = 0.03125
LOW = -1e30
VMEM = 56 * 1024 * 1024
PAD_ROWS = 64
Z_FIRST = 256
BID, MASK, CORE = 0, PAIRS, PAIRS + 4 * PAIRS
GROUPS, OWNERS = (0, 1, 3), (0, 1, 3)
NEAR = [(r, s) for r in GROUPS for s in OWNERS]
MIDDLE = [(2, s) for s in OWNERS]
LAST = [(r, 2) for r in (0, 1, 3, 2)]
WHOLE = pl.BlockSpec(memory_space=pltpu.VMEM)
SCALARS = pl.BlockSpec(memory_space=pltpu.SMEM)
OUTSIDE = pl.BlockSpec(memory_space=pltpu.HBM)


def spent(us):
    return pl.CostEstimate(flops=1000, bytes_accessed=1000 + 3_000_000 * us, transcendentals=0)


def score_kernel(groups, each, n_c, n_before, tab, seq, *refs):
    x_refs, refs = refs[: len(groups)], refs[len(groups) :]
    c_refs, refs = refs[:n_c], refs[n_c:]
    before, refs = refs[: 2 * n_before], refs[2 * n_before :]
    score_ref, m_ref, l_ref, xbuf, cbuf, sbuf, xsem, csem, ssem = refs
    block = cbuf.shape[1]
    total = each * len(groups)

    def score_copy(at, p):
        slot = lax.rem(at, 2)
        return pltpu.make_async_copy(sbuf.at[slot, p], score_ref.at[at, p], ssem.at[slot])

    def wait_scores(at):
        pair = SIDE * seq[2 * at] + seq[2 * at + 1]
        for p in range(4):

            @pl.when(tab[MASK + 4 * pair + p] == 1)
            def _():
                score_copy(at, p).wait()

    def start_c(at):
        r, owner = seq[2 * at], seq[2 * at + 1]
        slot = lax.rem(at, 2)
        bid = tab[BID + SIDE * r + owner]
        core = tab[CORE]
        side = jnp.where(owner == 2, bid // 4, jnp.where(owner == 1, 0, 1))
        beside = (owner == 1) | (owner == 3)
        wanted = (
            owner == 0,
            beside & (side == core),
            beside & (side != core),
            (owner == 2) & (side == core),
            (owner == 2) & (side != core),
        )
        for ref, here in zip(c_refs, wanted):

            @pl.when(here)
            def _():
                pltpu.make_async_copy(
                    ref.at[lax.rem(bid, ref.shape[0])], cbuf.at[slot], csem.at[slot]
                ).start()

    def x_copy(g):
        return pltpu.make_async_copy(x_refs[g], xbuf.at[g % 2], xsem.at[g % 2])

    x_copy(0).start()
    start_c(jnp.int32(0))
    for g, r in enumerate(groups):
        if g + 1 < len(groups):
            x_copy(g + 1).start()
        x_copy(g).wait()
        if n_before:
            source = 0 if r in GROUPS else 1
            place = GROUPS.index(r) if r in GROUPS else 0
            at = r
            m_ref[at] = before[2 * source][place]
            l_ref[at] = before[2 * source + 1][place]
        else:
            at = g
            m_ref[at] = jnp.full(m_ref.shape[1:], LOW, jnp.float32)
            l_ref[at] = jnp.zeros(l_ref.shape[1:], jnp.float32)

        def one_owner(j, carry, g=g, r=r, at=at):
            step = each * g + j
            cslot = lax.rem(step, 2)

            @pl.when(step < total - 1)
            def _():
                start_c(step + 1)

            @pl.when(step >= 2)
            def _():
                wait_scores(step - 2)

            pltpu.make_async_copy(cbuf.at[cslot], cbuf.at[cslot], csem.at[cslot]).wait()
            wide = cbuf[cslot].astype(jnp.float32)
            half_norm = 0.5 * jnp.sum(wide * wide, axis=1, keepdims=True)
            mask_at = MASK + 4 * (SIDE * r + seq[2 * step + 1])

            def one_block(p, carry):
                @pl.when(tab[mask_at + p] == 1)
                def _():
                    x = xbuf[g % 2, pl.ds(pl.multiple_of(p * block, block), block), :]
                    dots = lax.dot_general(
                        cbuf[cslot], x, (((1,), (1,)), ((), ())), preferred_element_type=jnp.float32
                    )
                    scores = (dots - half_norm) * inverse_temp
                    sbuf[cslot, p] = scores
                    score_copy(step, p).start()
                    old = m_ref[at, pl.ds(p, 1), :]
                    new = jnp.maximum(old, jnp.max(scores, axis=0, keepdims=True))
                    m_ref[at, pl.ds(p, 1), :] = new
                    l_ref[at, pl.ds(p, 1), :] = l_ref[at, pl.ds(p, 1), :] * jnp.exp(
                        old - new
                    ) + jnp.sum(jnp.exp(scores - new), axis=0, keepdims=True)

                return carry

            return lax.fori_loop(0, 4, one_block, carry)

        lax.fori_loop(0, each, one_owner, 0)
    for at in (total - 2, total - 1):
        wait_scores(at)


def score_call(tab, pairs, xs, cs, before=()):
    _, block, features = cs[0].shape
    groups = tuple(dict.fromkeys(r for r, _ in pairs))
    each = len(pairs) // len(groups)
    seq = jnp.array([v for pair in pairs for v in pair], jnp.int32)
    operands = [xs[r] for r in groups] + list(cs) + [v for pair in before for v in pair]
    stat = jax.ShapeDtypeStruct((SIDE if before else len(groups), 4, block), jnp.float32)
    return pl.pallas_call(
        functools.partial(score_kernel, groups, each, len(cs), len(before)),
        in_specs=[SCALARS] * 2
        + [OUTSIDE] * (len(groups) + len(cs))
        + [WHOLE] * (2 * len(before)),
        out_specs=[OUTSIDE, WHOLE, WHOLE],
        scratch_shapes=[
            pltpu.VMEM((2, *xs[0].shape), jnp.bfloat16),
            pltpu.VMEM((2, block, features), jnp.bfloat16),
            pltpu.VMEM((2, 4, block, block), jnp.float32),
            pltpu.SemaphoreType.DMA((2,)),
            pltpu.SemaphoreType.DMA((2,)),
            pltpu.SemaphoreType.DMA((2,)),
        ],
        out_shape=[
            jax.ShapeDtypeStruct((len(pairs), 4, block, block), jnp.float32),
            stat,
            stat,
        ],
        compiler_params=pltpu.CompilerParams(vmem_limit_bytes=VMEM),
        cost_estimate=spent(2 * len(pairs)),
        name="scores",
    )(tab, seq, *operands)


def sum_kernel(tab, *refs):
    x_refs, refs = refs[:SIDE], refs[SIDE:]
    near, middle, last, m_ref, r_ref, far_up, far_down, up, down, here, line = refs[:11]
    xbuf, acc, macc, total, stage, sbuf, xsem, sem, stage_sem, score_sem = refs[11:]
    block = acc.shape[0]

    def owner_of(at):
        j = at // SIDE
        return jnp.where(j == 0, 2, jnp.where(j == 1, 1, jnp.where(j == 2, 3, 0)))

    def start_scores(at):
        r, owner = lax.rem(at, SIDE), owner_of(at)
        group = jnp.where(r == 3, 2, r)
        place = jnp.where(owner == 3, 2, owner)
        slot = lax.rem(at, 2)
        far = owner == 2
        for ref, wanted, which in (
            (last, far, jnp.where(r == 2, 3, group)),
            (near, ~far & (r != 2), len(OWNERS) * group + place),
            (middle, ~far & (r == 2), place),
        ):
            for p in range(4):

                @pl.when(wanted & (tab[MASK + 4 * (SIDE * r + owner) + p] == 1))
                def _():
                    pltpu.make_async_copy(
                        ref.at[which, p], sbuf.at[slot, p], score_sem.at[slot]
                    ).start()

    def one_pair(r, owner, at, write):
        slot = r % 2

        @pl.when(at < PAIRS - 1)
        def _():
            start_scores(at + 1)

        for p in range(4):

            @pl.when(tab[MASK + 4 * (SIDE * r + owner) + p] == 1)
            def _():
                pltpu.make_async_copy(
                    last.at[0, p], sbuf.at[slot, p], score_sem.at[slot]
                ).wait()

        acc[...] = jnp.zeros(acc.shape, jnp.float32)
        macc[...] = jnp.zeros(macc.shape, jnp.float32)

        def one_block(p, carry):
            @pl.when(tab[MASK + 4 * (SIDE * r + owner) + p] == 1)
            def _():
                shares = (
                    jnp.exp(sbuf[slot, p] - m_ref[r, pl.ds(p, 1), :])
                    * r_ref[r, pl.ds(p, 1), :]
                )
                acc[...] += lax.dot_general(
                    shares.astype(jnp.bfloat16),
                    xbuf[r, pl.ds(pl.multiple_of(p * block, block), block), :],
                    (((1,), (0,)), ((), ())),
                    preferred_element_type=jnp.float32,
                )
                macc[...] += shares[:, :128] + shares[:, 128:]

            return carry

        lax.fori_loop(0, 4, one_block, 0)
        mass = jnp.sum(jnp.transpose(macc[...]), axis=0, keepdims=True)

        @pl.when(at >= 2)
        def _():
            stage_copy(here, 0, slot).wait()

        stage[slot, 0:block, :] = acc[:, Z_FIRST:].astype(jnp.bfloat16)
        stage[slot, block:, 0:block] = jnp.broadcast_to(mass, (16, block)).astype(jnp.bfloat16)
        stage[slot, block:, block:] = jnp.zeros((16, stage.shape[2] - block), jnp.bfloat16)
        write(slot)

    def stage_copy(out, at, slot):
        return pltpu.make_async_copy(stage.at[slot], out.at[at], stage_sem.at[slot])

    def add_line(r, owner, slot):
        bid = tab[BID + SIDE * r + owner]
        for i in range(block // 16):
            part = acc[16 * i : 16 * i + 16, :Z_FIRST].astype(jnp.bfloat16)
            total[slot, i, bid] += part.astype(jnp.float32)

    def line_copy(owner, slot):
        return pltpu.make_async_copy(total.at[slot], line.at[:, owner], sem.at[slot])

    def x_copy(r):
        return pltpu.make_async_copy(x_refs[r], xbuf.at[r], xsem.at[r])

    x_copy(0).start()
    start_scores(jnp.int32(0))
    total[0] = jnp.zeros(total.shape[1:], jnp.float32)
    for r in range(SIDE):
        if r + 1 < SIDE:
            x_copy(r + 1).start()
        x_copy(r).wait()
        out = (far_up, far_down)[r // 2]
        one_pair(r, 2, jnp.int32(r), lambda slot: stage_copy(out, r % 2, slot).start())
        add_line(r, 2, 0)
    line_copy(2, 0).start()

    def one_owner(j, carry):
        owner = owner_of(SIDE * (j + 1))
        slot = lax.rem(j + 1, 2)

        @pl.when(j >= 1)
        def _():
            line_copy(owner, slot).wait()

        total[slot] = jnp.zeros(total.shape[1:], jnp.float32)
        for r in range(SIDE):

            def write(slot):
                for i, out in enumerate((up, down, here)):

                    @pl.when(j == i)
                    def _():
                        stage_copy(out, r, slot).start()

            one_pair(r, owner, SIDE * (j + 1) + r, write)
            add_line(r, owner, slot)
        line_copy(owner, slot).start()
        return carry

    lax.fori_loop(0, 3, one_owner, 0)
    for slot in range(2):
        line_copy(0, slot).wait()
        stage_copy(here, 0, slot).wait()


def sum_call(tab, xs, scores, top, inverse, own_blocks):
    block = scores[0].shape[-1]
    features = xs[0].shape[1]
    parts = block // 16
    part = (own_blocks, 16, Z_FIRST)
    return pl.pallas_call(
        sum_kernel,
        in_specs=[SCALARS] + [OUTSIDE] * (SIDE + 3) + [WHOLE] * 2,
        out_specs=[OUTSIDE] * 6,
        scratch_shapes=[
            pltpu.VMEM((SIDE, *xs[0].shape), jnp.bfloat16),
            pltpu.VMEM((block, features), jnp.float32),
            pltpu.VMEM((block, 128), jnp.float32),
            pltpu.VMEM((2, parts, *part), jnp.float32),
            pltpu.VMEM((2, block + 16, features - Z_FIRST), jnp.bfloat16),
            pltpu.VMEM((2, 4, block, block), jnp.float32),
            pltpu.SemaphoreType.DMA((SIDE,)),
            pltpu.SemaphoreType.DMA((2,)),
            pltpu.SemaphoreType.DMA((2,)),
            pltpu.SemaphoreType.DMA((2,)),
        ],
        out_shape=[
            jax.ShapeDtypeStruct((n, block + 16, features - Z_FIRST), jnp.bfloat16)
            for n in (2, 2, 4, 4, 4)
        ]
        + [jax.ShapeDtypeStruct((parts, SIDE, *part), jnp.float32)],
        compiler_params=pltpu.CompilerParams(vmem_limit_bytes=VMEM),
        cost_estimate=spent(0),
        name="sums",
    )(tab, *[xs[r] for r in range(SIDE)], *scores, top, inverse)


def merge_kernel(ids, *refs):
    arrays, (out, buf, sem) = refs[:-3], refs[-3:]
    entries = [(ref, i) for ref in arrays for i in range(ref.shape[0])]

    def copy(k, slot):
        return pltpu.make_async_copy(buf.at[slot], out.at[k], sem.at[slot])

    def one_part(k, carry):
        slot = lax.rem(k, 2)

        @pl.when(k >= 2)
        def _():
            copy(k, slot).wait()

        buf[slot] = jnp.zeros(buf.shape[1:], jnp.float32)
        for e, (ref, i) in enumerate(entries):
            first = pl.multiple_of(32 * k + 16 * ids[len(entries)], 16)
            buf[slot, ids[e]] += ref[i, pl.ds(first, 16), :].astype(jnp.float32)
        copy(k, slot).start()
        return carry

    lax.fori_loop(0, out.shape[0], one_part, 0)
    for slot in range(2):
        copy(0, slot).wait()


def merge_call(ids, side, arrays, own_blocks):
    _, tall, features = arrays[0].shape
    part = (own_blocks, 16, features)
    return pl.pallas_call(
        merge_kernel,
        in_specs=[SCALARS] + [WHOLE] * len(arrays),
        out_specs=OUTSIDE,
        scratch_shapes=[pltpu.VMEM((2, *part), jnp.float32), pltpu.SemaphoreType.DMA((2,))],
        out_shape=jax.ShapeDtypeStruct((tall // 32, *part), jnp.float32),
        compiler_params=pltpu.CompilerParams(vmem_limit_bytes=VMEM // 3),
        cost_estimate=spent(0),
        name="merge",
    )(jnp.concatenate([ids, side.reshape(1)]), *arrays)


def mass_kernel(ids, *refs):
    arrays, out = refs[:-1], refs[-1]
    entries = [(ref, i) for ref in arrays for i in range(ref.shape[0])]
    out[...] = jnp.zeros(out.shape, jnp.float32)
    for e, (ref, i) in enumerate(entries):
        out[ids[e]] += ref[i][:, : out.shape[-1]].astype(jnp.float32)[0:8]


def mass_call(ids, arrays, own_blocks):
    _, tall, features = arrays[0].shape
    block = tall - 16
    return pl.pallas_call(
        mass_kernel,
        grid_spec=pltpu.PrefetchScalarGridSpec(
            num_scalar_prefetch=1,
            grid=(1,),
            in_specs=[
                pl.BlockSpec((a.shape[0], 16, features), lambda i, ids: (0, block // 16, 0))
                for a in arrays
            ],
            out_specs=pl.BlockSpec((own_blocks, 8, block), lambda i, ids: (0, 0, 0)),
        ),
        out_shape=jax.ShapeDtypeStruct((own_blocks, 8, block), jnp.float32),
        cost_estimate=spent(0),
        name="masses",
    )(ids, *arrays)


def pick_kernel(tab, low, high, beside, *refs):
    picked, part, same, xbuf, cbuf, xsem, csem = refs[-7:]
    share = part.shape[0]
    core = tab[CORE]
    pltpu.make_async_copy(beside.at[pl.ds(core * share, share)], cbuf, csem).start()
    for side, ref in enumerate((low, high)):

        @pl.when(core == side)
        def _():
            pltpu.make_async_copy(ref, xbuf, xsem).start()

    outward = ((xbuf, picked, xsem), (cbuf, part, csem))
    for buf, out, sem in outward:
        pltpu.make_async_copy(buf, buf, sem).wait()
        pltpu.make_async_copy(buf, out, sem).start()
    for buf, out, sem in outward:
        pltpu.make_async_copy(buf, out, sem).wait()


def pick_call(tab, low, high, beside):
    half = (beside.shape[0] // 2, *beside.shape[1:])
    return pl.pallas_call(
        pick_kernel,
        in_specs=[SCALARS] + [OUTSIDE] * 3,
        out_specs=[OUTSIDE] * 3,
        scratch_shapes=[
            pltpu.VMEM(low.shape, low.dtype),
            pltpu.VMEM(half, beside.dtype),
            pltpu.SemaphoreType.DMA,
            pltpu.SemaphoreType.DMA,
        ],
        out_shape=[
            jax.ShapeDtypeStruct(low.shape, low.dtype),
            jax.ShapeDtypeStruct(half, beside.dtype),
            jax.ShapeDtypeStruct(beside.shape, beside.dtype),
        ],
        input_output_aliases={3: 2},
        compiler_params=pltpu.CompilerParams(vmem_limit_bytes=VMEM),
        cost_estimate=spent(0),
        name="pick",
    )(tab, low, high, beside)


def shift_x(value, by):
    pairs = [
        (SIDE * x + y, SIDE * ((x + by) % SIDE) + y) for x in range(SIDE) for y in range(SIDE)
    ]
    return lax.ppermute(value, "cent", pairs)


def shift_y(value, by):
    pairs = [
        (SIDE * x + y, SIDE * x + (y + by) % SIDE) for x in range(SIDE) for y in range(SIDE)
    ]
    return lax.ppermute(value, "cent", pairs)


def from_either(value):
    n = PAIRS
    pairs = []
    for dp in range(16):
        for x in range(SIDE):
            for y in range(SIDE):
                source = (x + (-1 if dp % 2 == 0 else 1)) % SIDE
                pairs.append((dp * n + SIDE * source + y, dp * n + SIDE * x + y))
    return lax.ppermute(value, ("dp", "cent"), pairs)


def from_beside(value):
    n = PAIRS
    pairs = []
    for dp in range(16):
        for x in range(SIDE):
            for y in range(SIDE):
                source = (y + (1 if dp % 2 == 0 else -1)) % SIDE
                pairs.append((dp * n + SIDE * x + source, dp * n + SIDE * x + y))
    return lax.ppermute(value, ("dp", "cent"), pairs)


def swap_core(value):
    return lax.ppermute(value, "dp", [(i, i ^ 1) for i in range(16)])


def nothing(*arrays):
    return sum(jnp.minimum(jnp.abs(a[0, 0]), 0) for a in arrays)


def tables(candidates, own_blocks):
    place = lax.axis_index("cent")
    x, y = place // SIDE, place % SIDE
    core = (lax.axis_index("dp") % 2).astype(jnp.int32)
    n, each = candidates.shape
    padded = jnp.pad(candidates, ((0, PAD_ROWS - n), (0, 256 - each)))
    every = lax.all_gather(padded, "cent", axis=0, tiled=True)
    every = every.reshape(SIDE, SIDE, PAD_ROWS, 256)[:, :, :n, :each]
    near = jnp.roll(every, (-x, -y), axis=(0, 1))
    owner, local = near // own_blocks, near % own_blocks
    line = SIDE * x + (y + jnp.arange(SIDE, dtype=jnp.int32)) % SIDE
    named = owner[:, 0][:, None] == line[None, :, None, None]
    bid = jnp.max(jnp.where(named, local[:, 0][:, None], 0), axis=(2, 3)).astype(jnp.int32)
    mask = jnp.any(named, axis=3).astype(jnp.int32)
    tab = jnp.concatenate([bid.reshape(-1), mask.reshape(-1), core.reshape(1)])
    mine = jnp.max(jnp.where(owner == place, local, 0), axis=(2, 3)).astype(jnp.int32)
    return tab, mine, core


def per_device(points, candidates, centroids):
    own_blocks, block, features = centroids.shape
    stripe = lax.axis_size("dp")
    rows_each = block // stripe
    dp_place = lax.axis_index("dp")
    tab, mine, core = tables(candidates, own_blocks)

    x3, x1 = shift_x(points, 1), shift_x(points, -1)
    handed, part, beside = pick_call(tab, x3, x1, from_beside(centroids))
    x2 = from_either(handed)
    opposite = from_beside(part)
    xs = {0: points, 1: x1, 2: x2, 3: x3}
    cs = [centroids, beside, swap_core(beside)]
    near, *near_stats = score_call(tab, NEAR, xs, cs)
    opposite += nothing(near_stats[0][0]).astype(opposite.dtype)
    middle, *middle_stats = score_call(tab, MIDDLE, xs, cs)
    cs += [opposite, swap_core(opposite)]
    last, top, total = score_call(tab, LAST, xs, cs, (near_stats, middle_stats))

    stats = jnp.stack([top, total])
    tops, totals = [top], [total]
    for by in (1, 2, 3):
        moved = jnp.roll(shift_x(stats, -by), by, axis=1)
        tops.append(moved[0])
        totals.append(moved[1])
    highest = functools.reduce(jnp.maximum, tops)
    whole = sum(t * jnp.exp(m - highest) for m, t in zip(tops, totals))
    inverse = 1.0 / whole

    lines = [[2 * z + c for z in range(stripe // 2)] for c in range(2)]

    def over_z(sums, other):
        both = sums + swap_core(other)
        return lax.psum_scatter(
            both, "dp", scatter_dimension=0, axis_index_groups=lines, tiled=True
        )[0]

    far_up, far_down, up, down, here, line = sum_call(
        tab, xs, (near, middle, last), highest, inverse, own_blocks
    )
    line = lax.psum_scatter(line, "dp", scatter_dimension=0, tiled=True)[0]
    far_up, far_down = shift_y(far_up, 1), shift_y(far_down, -1)
    up, down = shift_y(up, 1), shift_y(down, -1)
    far_up, far_down = shift_y(far_up, 1), shift_y(far_down, -1)
    ids = jnp.concatenate([mine[:, 0], mine[:, 2], mine[:, 3], mine[:, 1]])
    arrays = (here, far_up, far_down, up, down)
    other = merge_call(ids, 1 - core, arrays, own_blocks)
    sums = over_z(merge_call(ids, core, arrays, own_blocks), other)
    line = line[0] + shift_y(line[1], 1) + shift_y(line[2], 2) + shift_y(line[3], -1)
    mass = mass_call(ids, arrays, own_blocks)[:, 0, :]
    mass = mass.reshape(own_blocks, stripe, rows_each).transpose(1, 0, 2)
    mass = lax.all_to_all(mass, "dp", split_axis=0, concat_axis=0, tiled=True)
    new_mass = jnp.sum(mass, axis=0)
    previous = lax.dynamic_slice_in_dim(centroids, dp_place * rows_each, rows_each, 1).astype(
        jnp.float32
    )
    new_sums = jnp.concatenate([line, sums], axis=2)
    return (new_sums + previous) / (new_mass + 1.0)[:, :, None], new_mass


def solution(mesh):
    in_specs = (P(("dp", "cent"), None), P(("dp", "cent"), None), P("cent", None, None))
    out_specs = (P("cent", "dp", None), P("cent", "dp"))
    return jax.shard_map(
        per_device, mesh=mesh, in_specs=in_specs, out_specs=out_specs, check_vma=False
    )
```

```python
import functools

import jax
import jax.numpy as jnp
from jax import lax
from jax.experimental import pallas as pl
from jax.experimental.pallas import tpu as pltpu
from jax.sharding import PartitionSpec as P

SIDE = 4
PAIRS = SIDE * SIDE
inverse_temp = 0.03125
LOW = -1e30
VMEM = 56 * 1024 * 1024
PAD_ROWS = 64
Z_FIRST = 384
BID, MASK, CORE = 0, PAIRS, PAIRS + 4 * PAIRS
GROUPS, OWNERS = (0, 1, 3), (0, 1, 3)
NEAR = [(r, s) for r in GROUPS for s in OWNERS]
MIDDLE = [(2, s) for s in OWNERS]
LAST = [(r, 2) for r in (0, 1, 3, 2)]
WHOLE = pl.BlockSpec(memory_space=pltpu.VMEM)
SCALARS = pl.BlockSpec(memory_space=pltpu.SMEM)
OUTSIDE = pl.BlockSpec(memory_space=pltpu.HBM)


def spent(us):
    return pl.CostEstimate(flops=1000, bytes_accessed=1000 + 3_000_000 * us, transcendentals=0)


def score_kernel(groups, each, n_c, n_before, tab, seq, *refs):
    x_refs, refs = refs[: len(groups)], refs[len(groups) :]
    c_refs, refs = refs[:n_c], refs[n_c:]
    before, refs = refs[: 2 * n_before], refs[2 * n_before :]
    score_ref, m_ref, l_ref, xbuf, cbuf, sbuf, xsem, csem, ssem = refs
    block = cbuf.shape[1]
    total = each * len(groups)

    def score_copy(at, p):
        slot = lax.rem(at, 2)
        return pltpu.make_async_copy(sbuf.at[slot, p], score_ref.at[at, p], ssem.at[slot])

    def wait_scores(at):
        pair = SIDE * seq[2 * at] + seq[2 * at + 1]
        for p in range(4):

            @pl.when(tab[MASK + 4 * pair + p] == 1)
            def _():
                score_copy(at, p).wait()

    def start_c(at):
        r, owner = seq[2 * at], seq[2 * at + 1]
        slot = lax.rem(at, 2)
        bid = tab[BID + SIDE * r + owner]
        core = tab[CORE]
        side = jnp.where(owner == 2, bid // 4, jnp.where(owner == 1, 0, 1))
        beside = (owner == 1) | (owner == 3)
        wanted = (
            owner == 0,
            beside & (side == core),
            beside & (side != core),
            (owner == 2) & (side == core),
            (owner == 2) & (side != core),
        )
        for ref, here in zip(c_refs, wanted):

            @pl.when(here)
            def _():
                pltpu.make_async_copy(
                    ref.at[lax.rem(bid, ref.shape[0])], cbuf.at[slot], csem.at[slot]
                ).start()

    def x_copy(g):
        return pltpu.make_async_copy(x_refs[g], xbuf.at[g % 2], xsem.at[g % 2])

    x_copy(0).start()
    start_c(jnp.int32(0))
    for g, r in enumerate(groups):
        if g + 1 < len(groups):
            x_copy(g + 1).start()
        x_copy(g).wait()
        if n_before:
            source = 0 if r in GROUPS else 1
            place = GROUPS.index(r) if r in GROUPS else 0
            at = r
            m_ref[at] = before[2 * source][place]
            l_ref[at] = before[2 * source + 1][place]
        else:
            at = g
            m_ref[at] = jnp.full(m_ref.shape[1:], LOW, jnp.float32)
            l_ref[at] = jnp.zeros(l_ref.shape[1:], jnp.float32)

        def one_owner(j, carry, g=g, r=r, at=at):
            step = each * g + j
            cslot = lax.rem(step, 2)

            @pl.when(step < total - 1)
            def _():
                start_c(step + 1)

            @pl.when(step >= 2)
            def _():
                wait_scores(step - 2)

            pltpu.make_async_copy(cbuf.at[cslot], cbuf.at[cslot], csem.at[cslot]).wait()
            wide = cbuf[cslot].astype(jnp.float32)
            half_norm = 0.5 * jnp.sum(wide * wide, axis=1, keepdims=True)
            mask_at = MASK + 4 * (SIDE * r + seq[2 * step + 1])

            def one_block(p, carry):
                @pl.when(tab[mask_at + p] == 1)
                def _():
                    x = xbuf[g % 2, pl.ds(pl.multiple_of(p * block, block), block), :]
                    dots = lax.dot_general(
                        cbuf[cslot], x, (((1,), (1,)), ((), ())), preferred_element_type=jnp.float32
                    )
                    scores = (dots - half_norm) * inverse_temp
                    sbuf[cslot, p] = scores
                    score_copy(step, p).start()
                    old = m_ref[at, pl.ds(p, 1), :]
                    new = jnp.maximum(old, jnp.max(scores, axis=0, keepdims=True))
                    m_ref[at, pl.ds(p, 1), :] = new
                    l_ref[at, pl.ds(p, 1), :] = l_ref[at, pl.ds(p, 1), :] * jnp.exp(
                        old - new
                    ) + jnp.sum(jnp.exp(scores - new), axis=0, keepdims=True)

                return carry

            return lax.fori_loop(0, 4, one_block, carry)

        lax.fori_loop(0, each, one_owner, 0)
    for at in (total - 2, total - 1):
        wait_scores(at)


def score_call(tab, pairs, xs, cs, before=()):
    _, block, features = cs[0].shape
    groups = tuple(dict.fromkeys(r for r, _ in pairs))
    each = len(pairs) // len(groups)
    seq = jnp.array([v for pair in pairs for v in pair], jnp.int32)
    operands = [xs[r] for r in groups] + list(cs) + [v for pair in before for v in pair]
    stat = jax.ShapeDtypeStruct((SIDE if before else len(groups), 4, block), jnp.float32)
    return pl.pallas_call(
        functools.partial(score_kernel, groups, each, len(cs), len(before)),
        in_specs=[SCALARS] * 2
        + [OUTSIDE] * (len(groups) + len(cs))
        + [WHOLE] * (2 * len(before)),
        out_specs=[OUTSIDE, WHOLE, WHOLE],
        scratch_shapes=[
            pltpu.VMEM((2, *xs[0].shape), jnp.bfloat16),
            pltpu.VMEM((2, block, features), jnp.bfloat16),
            pltpu.VMEM((2, 4, block, block), jnp.float32),
            pltpu.SemaphoreType.DMA((2,)),
            pltpu.SemaphoreType.DMA((2,)),
            pltpu.SemaphoreType.DMA((2,)),
        ],
        out_shape=[
            jax.ShapeDtypeStruct((len(pairs), 4, block, block), jnp.float32),
            stat,
            stat,
        ],
        compiler_params=pltpu.CompilerParams(vmem_limit_bytes=VMEM),
        cost_estimate=spent(2 * len(pairs)),
        name="scores",
    )(tab, seq, *operands)


def sum_kernel(tab, *refs):
    x_refs, refs = refs[:SIDE], refs[SIDE:]
    near, middle, last, m_ref, r_ref, far_up, far_down, up, down, here, line = refs[:11]
    xbuf, acc, macc, total, stage, sbuf, xsem, sem, stage_sem, score_sem = refs[11:]
    block = acc.shape[0]

    def owner_of(at):
        j = at // SIDE
        return jnp.where(j == 0, 2, jnp.where(j == 1, 1, jnp.where(j == 2, 3, 0)))

    def start_scores(at):
        r, owner = lax.rem(at, SIDE), owner_of(at)
        group = jnp.where(r == 3, 2, r)
        place = jnp.where(owner == 3, 2, owner)
        slot = lax.rem(at, 2)
        far = owner == 2
        for ref, wanted, which in (
            (last, far, jnp.where(r == 2, 3, group)),
            (near, ~far & (r != 2), len(OWNERS) * group + place),
            (middle, ~far & (r == 2), place),
        ):
            for p in range(4):

                @pl.when(wanted & (tab[MASK + 4 * (SIDE * r + owner) + p] == 1))
                def _():
                    pltpu.make_async_copy(
                        ref.at[which, p], sbuf.at[slot, p], score_sem.at[slot]
                    ).start()

    def one_pair(r, owner, at, write):
        slot = r % 2

        @pl.when(at < PAIRS - 1)
        def _():
            start_scores(at + 1)

        for p in range(4):

            @pl.when(tab[MASK + 4 * (SIDE * r + owner) + p] == 1)
            def _():
                pltpu.make_async_copy(
                    last.at[0, p], sbuf.at[slot, p], score_sem.at[slot]
                ).wait()

        acc[...] = jnp.zeros(acc.shape, jnp.float32)
        macc[...] = jnp.zeros(macc.shape, jnp.float32)

        def one_block(p, carry):
            @pl.when(tab[MASK + 4 * (SIDE * r + owner) + p] == 1)
            def _():
                shares = (
                    jnp.exp(sbuf[slot, p] - m_ref[r, pl.ds(p, 1), :])
                    * r_ref[r, pl.ds(p, 1), :]
                )
                acc[...] += lax.dot_general(
                    shares.astype(jnp.bfloat16),
                    xbuf[r, pl.ds(pl.multiple_of(p * block, block), block), :],
                    (((1,), (0,)), ((), ())),
                    preferred_element_type=jnp.float32,
                )
                macc[...] += shares[:, :128] + shares[:, 128:]

            return carry

        lax.fori_loop(0, 4, one_block, 0)
        mass = jnp.sum(jnp.transpose(macc[...]), axis=0, keepdims=True)

        @pl.when(at >= 2)
        def _():
            stage_copy(here, 0, slot).wait()

        stage[slot, 0:block, :] = acc[:, Z_FIRST:].astype(jnp.bfloat16)
        stage[slot, block:, 0:block] = jnp.broadcast_to(mass, (16, block)).astype(jnp.bfloat16)
        stage[slot, block:, block:] = jnp.zeros((16, stage.shape[2] - block), jnp.bfloat16)
        write(slot)

    def stage_copy(out, at, slot):
        return pltpu.make_async_copy(stage.at[slot], out.at[at], stage_sem.at[slot])

    def add_line(r, owner, slot):
        bid = tab[BID + SIDE * r + owner]
        for i in range(block // 16):
            part = acc[16 * i : 16 * i + 16, :Z_FIRST].astype(jnp.bfloat16)
            total[slot, i, bid] += part.astype(jnp.float32)

    def line_copy(owner, slot):
        return pltpu.make_async_copy(total.at[slot], line.at[:, owner], sem.at[slot])

    def x_copy(r):
        return pltpu.make_async_copy(x_refs[r], xbuf.at[r], xsem.at[r])

    x_copy(0).start()
    start_scores(jnp.int32(0))
    total[0] = jnp.zeros(total.shape[1:], jnp.float32)
    for r in range(SIDE):
        if r + 1 < SIDE:
            x_copy(r + 1).start()
        x_copy(r).wait()
        out = (far_up, far_down)[r // 2]
        one_pair(r, 2, jnp.int32(r), lambda slot: stage_copy(out, r % 2, slot).start())
        add_line(r, 2, 0)
    line_copy(2, 0).start()

    def one_owner(j, carry):
        owner = owner_of(SIDE * (j + 1))
        slot = lax.rem(j + 1, 2)

        @pl.when(j >= 1)
        def _():
            line_copy(owner, slot).wait()

        total[slot] = jnp.zeros(total.shape[1:], jnp.float32)
        for r in range(SIDE):

            def write(slot):
                for i, out in enumerate((up, down, here)):

                    @pl.when(j == i)
                    def _():
                        stage_copy(out, r, slot).start()

            one_pair(r, owner, SIDE * (j + 1) + r, write)
            add_line(r, owner, slot)
        line_copy(owner, slot).start()
        return carry

    lax.fori_loop(0, 3, one_owner, 0)
    for slot in range(2):
        line_copy(0, slot).wait()
        stage_copy(here, 0, slot).wait()


def sum_call(tab, xs, scores, top, inverse, own_blocks):
    block = scores[0].shape[-1]
    features = xs[0].shape[1]
    parts = block // 16
    part = (own_blocks, 16, Z_FIRST)
    return pl.pallas_call(
        sum_kernel,
        in_specs=[SCALARS] + [OUTSIDE] * (SIDE + 3) + [WHOLE] * 2,
        out_specs=[OUTSIDE] * 6,
        scratch_shapes=[
            pltpu.VMEM((SIDE, *xs[0].shape), jnp.bfloat16),
            pltpu.VMEM((block, features), jnp.float32),
            pltpu.VMEM((block, 128), jnp.float32),
            pltpu.VMEM((2, parts, *part), jnp.float32),
            pltpu.VMEM((2, block + 16, features - Z_FIRST), jnp.bfloat16),
            pltpu.VMEM((2, 4, block, block), jnp.float32),
            pltpu.SemaphoreType.DMA((SIDE,)),
            pltpu.SemaphoreType.DMA((2,)),
            pltpu.SemaphoreType.DMA((2,)),
            pltpu.SemaphoreType.DMA((2,)),
        ],
        out_shape=[
            jax.ShapeDtypeStruct((n, block + 16, features - Z_FIRST), jnp.bfloat16)
            for n in (2, 2, 4, 4, 4)
        ]
        + [jax.ShapeDtypeStruct((parts, SIDE, *part), jnp.float32)],
        compiler_params=pltpu.CompilerParams(vmem_limit_bytes=VMEM),
        cost_estimate=spent(0),
        name="sums",
    )(tab, *[xs[r] for r in range(SIDE)], *scores, top, inverse)


def merge_kernel(ids, *refs):
    arrays, (out, buf, odd, sem) = refs[:-4], refs[-4:]
    entries = [(ref, i) for ref in arrays for i in range(ref.shape[0])]

    def copy(k, slot):
        return pltpu.make_async_copy(buf.at[slot], out.at[k], sem.at[slot])

    def one_part(k, carry):
        slot = lax.rem(k, 2)

        @pl.when(k >= 2)
        def _():
            copy(k, slot).wait()

        first = pl.multiple_of(32 * k + 16 * ids[len(entries)], 16)
        buf[slot] = jnp.zeros(buf.shape[1:], jnp.float32)
        odd[...] = jnp.zeros(odd.shape, jnp.float32)
        for e, (ref, i) in enumerate(entries):
            rows = ref[i, pl.ds(first, 16), :].astype(jnp.float32)
            if e % 2:
                odd[ids[e]] += rows
            else:
                buf[slot, ids[e]] += rows
        buf[slot] += odd[...]
        copy(k, slot).start()
        return carry

    lax.fori_loop(0, out.shape[0], one_part, 0)
    for slot in range(2):
        copy(0, slot).wait()


def merge_call(ids, side, arrays, own_blocks):
    _, tall, features = arrays[0].shape
    part = (own_blocks, 16, features)
    return pl.pallas_call(
        merge_kernel,
        in_specs=[SCALARS] + [WHOLE] * len(arrays),
        out_specs=OUTSIDE,
        scratch_shapes=[
            pltpu.VMEM((2, *part), jnp.float32),
            pltpu.VMEM(part, jnp.float32),
            pltpu.SemaphoreType.DMA((2,)),
        ],
        out_shape=jax.ShapeDtypeStruct((tall // 32, *part), jnp.float32),
        compiler_params=pltpu.CompilerParams(vmem_limit_bytes=VMEM // 3),
        cost_estimate=spent(0),
        name="merge",
    )(jnp.concatenate([ids, side.reshape(1)]), *arrays)


def mass_kernel(ids, *refs):
    arrays, out = refs[:-1], refs[-1]
    entries = [(ref, i) for ref in arrays for i in range(ref.shape[0])]
    out[...] = jnp.zeros(out.shape, jnp.float32)
    for e, (ref, i) in enumerate(entries):
        out[ids[e]] += ref[i][:, : out.shape[-1]].astype(jnp.float32)[0:8]


def mass_call(ids, arrays, own_blocks):
    _, tall, features = arrays[0].shape
    block = tall - 16
    return pl.pallas_call(
        mass_kernel,
        grid_spec=pltpu.PrefetchScalarGridSpec(
            num_scalar_prefetch=1,
            grid=(1,),
            in_specs=[
                pl.BlockSpec((a.shape[0], 16, features), lambda i, ids: (0, block // 16, 0))
                for a in arrays
            ],
            out_specs=pl.BlockSpec((own_blocks, 8, block), lambda i, ids: (0, 0, 0)),
        ),
        out_shape=jax.ShapeDtypeStruct((own_blocks, 8, block), jnp.float32),
        cost_estimate=spent(0),
        name="masses",
    )(ids, *arrays)


def pick_kernel(tab, low, high, beside, *refs):
    picked, part, same, xbuf, cbuf, xsem, csem = refs[-7:]
    share = part.shape[0]
    core = tab[CORE]
    pltpu.make_async_copy(beside.at[pl.ds(core * share, share)], cbuf, csem).start()
    for side, ref in enumerate((low, high)):

        @pl.when(core == side)
        def _():
            pltpu.make_async_copy(ref, xbuf, xsem).start()

    outward = ((xbuf, picked, xsem), (cbuf, part, csem))
    for buf, out, sem in outward:
        pltpu.make_async_copy(buf, buf, sem).wait()
        pltpu.make_async_copy(buf, out, sem).start()
    for buf, out, sem in outward:
        pltpu.make_async_copy(buf, out, sem).wait()


def pick_call(tab, low, high, beside):
    half = (beside.shape[0] // 2, *beside.shape[1:])
    return pl.pallas_call(
        pick_kernel,
        in_specs=[SCALARS] + [OUTSIDE] * 3,
        out_specs=[OUTSIDE] * 3,
        scratch_shapes=[
            pltpu.VMEM(low.shape, low.dtype),
            pltpu.VMEM(half, beside.dtype),
            pltpu.SemaphoreType.DMA,
            pltpu.SemaphoreType.DMA,
        ],
        out_shape=[
            jax.ShapeDtypeStruct(low.shape, low.dtype),
            jax.ShapeDtypeStruct(half, beside.dtype),
            jax.ShapeDtypeStruct(beside.shape, beside.dtype),
        ],
        input_output_aliases={3: 2},
        compiler_params=pltpu.CompilerParams(vmem_limit_bytes=VMEM),
        cost_estimate=spent(0),
        name="pick",
    )(tab, low, high, beside)


def shift_x(value, by):
    pairs = [
        (SIDE * x + y, SIDE * ((x + by) % SIDE) + y) for x in range(SIDE) for y in range(SIDE)
    ]
    return lax.ppermute(value, "cent", pairs)


def shift_y(value, by):
    pairs = [
        (SIDE * x + y, SIDE * x + (y + by) % SIDE) for x in range(SIDE) for y in range(SIDE)
    ]
    return lax.ppermute(value, "cent", pairs)


def from_either(value):
    n = PAIRS
    pairs = []
    for dp in range(16):
        for x in range(SIDE):
            for y in range(SIDE):
                source = (x + (-1 if dp % 2 == 0 else 1)) % SIDE
                pairs.append((dp * n + SIDE * source + y, dp * n + SIDE * x + y))
    return lax.ppermute(value, ("dp", "cent"), pairs)


def from_beside(value):
    n = PAIRS
    pairs = []
    for dp in range(16):
        for x in range(SIDE):
            for y in range(SIDE):
                source = (y + (1 if dp % 2 == 0 else -1)) % SIDE
                pairs.append((dp * n + SIDE * x + source, dp * n + SIDE * x + y))
    return lax.ppermute(value, ("dp", "cent"), pairs)


def swap_core(value):
    return lax.ppermute(value, "dp", [(i, i ^ 1) for i in range(16)])


def nothing(*arrays):
    return sum(jnp.minimum(jnp.abs(a[0, 0]), 0) for a in arrays)


def tables(candidates, own_blocks):
    place = lax.axis_index("cent")
    x, y = place // SIDE, place % SIDE
    core = (lax.axis_index("dp") % 2).astype(jnp.int32)
    n, each = candidates.shape
    padded = jnp.pad(candidates, ((0, PAD_ROWS - n), (0, 256 - each)))
    every = lax.all_gather(padded, "cent", axis=0, tiled=True)
    every = every.reshape(SIDE, SIDE, PAD_ROWS, 256)[:, :, :n, :each]
    near = jnp.roll(every, (-x, -y), axis=(0, 1))
    owner, local = near // own_blocks, near % own_blocks
    line = SIDE * x + (y + jnp.arange(SIDE, dtype=jnp.int32)) % SIDE
    named = owner[:, 0][:, None] == line[None, :, None, None]
    bid = jnp.max(jnp.where(named, local[:, 0][:, None], 0), axis=(2, 3)).astype(jnp.int32)
    mask = jnp.any(named, axis=3).astype(jnp.int32)
    tab = jnp.concatenate([bid.reshape(-1), mask.reshape(-1), core.reshape(1)])
    mine = jnp.max(jnp.where(owner == place, local, 0), axis=(2, 3)).astype(jnp.int32)
    return tab, mine, core


def per_device(points, candidates, centroids):
    own_blocks, block, features = centroids.shape
    stripe = lax.axis_size("dp")
    rows_each = block // stripe
    dp_place = lax.axis_index("dp")
    tab, mine, core = tables(candidates, own_blocks)

    x3, x1 = shift_x(points, 1), shift_x(points, -1)
    handed, part, beside = pick_call(tab, x3, x1, from_beside(centroids))
    x2 = from_either(handed)
    opposite = from_beside(part)
    xs = {0: points, 1: x1, 2: x2, 3: x3}
    cs = [centroids, beside, swap_core(beside)]
    near, *near_stats = score_call(tab, NEAR, xs, cs)
    opposite += nothing(near_stats[0][0]).astype(opposite.dtype)
    middle, *middle_stats = score_call(tab, MIDDLE, xs, cs)
    cs += [opposite, swap_core(opposite)]
    last, top, total = score_call(tab, LAST, xs, cs, (near_stats, middle_stats))

    stats = jnp.stack([top, total])
    tops, totals = [top], [total]
    for by in (1, 2, 3):
        moved = jnp.roll(shift_x(stats, -by), by, axis=1)
        tops.append(moved[0])
        totals.append(moved[1])
    highest = functools.reduce(jnp.maximum, tops)
    whole = sum(t * jnp.exp(m - highest) for m, t in zip(tops, totals))
    inverse = 1.0 / whole

    lines = [[2 * z + c for z in range(stripe // 2)] for c in range(2)]

    def over_z(sums, other):
        both = sums + swap_core(other)
        return lax.psum_scatter(
            both, "dp", scatter_dimension=0, axis_index_groups=lines, tiled=True
        )[0]

    far_up, far_down, up, down, here, line = sum_call(
        tab, xs, (near, middle, last), highest, inverse, own_blocks
    )
    line = lax.psum_scatter(line, "dp", scatter_dimension=0, tiled=True)[0]
    far_up, far_down = shift_y(far_up, 1), shift_y(far_down, -1)
    up, down = shift_y(up, 1), shift_y(down, -1)
    far_up, far_down = shift_y(far_up, 1), shift_y(far_down, -1)
    ids = jnp.concatenate([mine[:, 0], mine[:, 2], mine[:, 3], mine[:, 1]])
    arrays = (here, far_up, far_down, up, down)
    other = merge_call(ids, 1 - core, arrays, own_blocks)
    sums = over_z(merge_call(ids, core, arrays, own_blocks), other)
    line = line[0] + shift_y(line[1], 1) + shift_y(line[2], 2) + shift_y(line[3], -1)
    mass = mass_call(ids, arrays, own_blocks)[:, 0, :]
    mass = mass.reshape(own_blocks, stripe, rows_each).transpose(1, 0, 2)
    mass = lax.all_to_all(mass, "dp", split_axis=0, concat_axis=0, tiled=True)
    new_mass = jnp.sum(mass, axis=0)
    previous = lax.dynamic_slice_in_dim(centroids, dp_place * rows_each, rows_each, 1).astype(
        jnp.float32
    )
    new_sums = jnp.concatenate([line, sums], axis=2)
    return (new_sums + previous) / (new_mass + 1.0)[:, :, None], new_mass


def solution(mesh):
    in_specs = (P(("dp", "cent"), None), P(("dp", "cent"), None), P("cent", None, None))
    out_specs = (P("cent", "dp", None), P("cent", "dp"))
    return jax.shard_map(
        per_device, mesh=mesh, in_specs=in_specs, out_specs=out_specs, check_vma=False
    )
```

```python
import functools

import jax
import jax.numpy as jnp
from jax import lax
from jax.experimental import pallas as pl
from jax.experimental.pallas import tpu as pltpu
from jax.sharding import PartitionSpec as P

SIDE = 4
PAIRS = SIDE * SIDE
inverse_temp = 0.03125
LOW = -1e30
VMEM = 56 * 1024 * 1024
PAD_ROWS = 64
Z_FIRST = 384
BID, MASK, CORE = 0, PAIRS, PAIRS + 4 * PAIRS
GROUPS, OWNERS = (0, 1, 3), (0, 1, 3)
NEAR = [(r, s) for r in GROUPS for s in OWNERS]
MIDDLE = [(2, s) for s in OWNERS]
LAST = [(r, 2) for r in (0, 1, 3, 2)]
WHOLE = pl.BlockSpec(memory_space=pltpu.VMEM)
SCALARS = pl.BlockSpec(memory_space=pltpu.SMEM)
OUTSIDE = pl.BlockSpec(memory_space=pltpu.HBM)


def spent(us):
    return pl.CostEstimate(flops=1000, bytes_accessed=1000 + 3_000_000 * us, transcendentals=0)


def score_kernel(groups, each, n_c, n_before, tab, seq, *refs):
    x_refs, refs = refs[: len(groups)], refs[len(groups) :]
    c_refs, refs = refs[:n_c], refs[n_c:]
    before, refs = refs[:n_before], refs[n_before:]
    score_ref, stat_ref, xbuf, cbuf, sbuf, xsem, csem, ssem = refs
    block = cbuf.shape[1]
    total = each * len(groups)

    def score_copy(at, p):
        slot = lax.rem(at, 2)
        return pltpu.make_async_copy(sbuf.at[slot, p], score_ref.at[at, p], ssem.at[slot])

    def wait_scores(at):
        pair = SIDE * seq[2 * at] + seq[2 * at + 1]
        for p in range(4):

            @pl.when(tab[MASK + 4 * pair + p] == 1)
            def _():
                score_copy(at, p).wait()

    def start_c(at):
        r, owner = seq[2 * at], seq[2 * at + 1]
        slot = lax.rem(at, 2)
        bid = tab[BID + SIDE * r + owner]
        core = tab[CORE]
        side = jnp.where(owner == 2, bid // 4, jnp.where(owner == 1, 0, 1))
        beside = (owner == 1) | (owner == 3)
        wanted = (
            owner == 0,
            beside & (side == core),
            beside & (side != core),
            (owner == 2) & (side == core),
            (owner == 2) & (side != core),
        )
        for ref, here in zip(c_refs, wanted):

            @pl.when(here)
            def _():
                pltpu.make_async_copy(
                    ref.at[lax.rem(bid, ref.shape[0])], cbuf.at[slot], csem.at[slot]
                ).start()

    def x_copy(g):
        return pltpu.make_async_copy(x_refs[g], xbuf.at[g % 2], xsem.at[g % 2])

    x_copy(0).start()
    start_c(jnp.int32(0))
    for g, r in enumerate(groups):
        if g + 1 < len(groups):
            x_copy(g + 1).start()
        x_copy(g).wait()
        if n_before:
            source = 0 if r in GROUPS else 1
            place = GROUPS.index(r) if r in GROUPS else 0
            at = r
            stat_ref[0, at] = before[source][0, place]
            stat_ref[1, at] = before[source][1, place]
        else:
            at = g
            stat_ref[0, at] = jnp.full(stat_ref.shape[2:], LOW, jnp.float32)
            stat_ref[1, at] = jnp.zeros(stat_ref.shape[2:], jnp.float32)

        def one_owner(j, carry, g=g, r=r, at=at):
            step = each * g + j
            cslot = lax.rem(step, 2)

            @pl.when(step < total - 1)
            def _():
                start_c(step + 1)

            @pl.when(step >= 2)
            def _():
                wait_scores(step - 2)

            pltpu.make_async_copy(cbuf.at[cslot], cbuf.at[cslot], csem.at[cslot]).wait()
            wide = cbuf[cslot].astype(jnp.float32)
            half_norm = 0.5 * jnp.sum(wide * wide, axis=1, keepdims=True)
            mask_at = MASK + 4 * (SIDE * r + seq[2 * step + 1])

            def one_block(p, carry):
                @pl.when(tab[mask_at + p] == 1)
                def _():
                    x = xbuf[g % 2, pl.ds(pl.multiple_of(p * block, block), block), :]
                    dots = lax.dot_general(
                        cbuf[cslot], x, (((1,), (1,)), ((), ())), preferred_element_type=jnp.float32
                    )
                    scores = (dots - half_norm) * inverse_temp
                    sbuf[cslot, p] = scores
                    score_copy(step, p).start()
                    old = stat_ref[0, at, pl.ds(p, 1), :]
                    new = jnp.maximum(old, jnp.max(scores, axis=0, keepdims=True))
                    stat_ref[0, at, pl.ds(p, 1), :] = new
                    stat_ref[1, at, pl.ds(p, 1), :] = stat_ref[1, at, pl.ds(p, 1), :] * jnp.exp(
                        old - new
                    ) + jnp.sum(jnp.exp(scores - new), axis=0, keepdims=True)

                return carry

            return lax.fori_loop(0, 4, one_block, carry)

        lax.fori_loop(0, each, one_owner, 0)
    for at in (total - 2, total - 1):
        wait_scores(at)


def score_call(tab, pairs, xs, cs, before=()):
    _, block, features = cs[0].shape
    groups = tuple(dict.fromkeys(r for r, _ in pairs))
    each = len(pairs) // len(groups)
    seq = jnp.array([v for pair in pairs for v in pair], jnp.int32)
    operands = [xs[r] for r in groups] + list(cs) + list(before)
    stat = jax.ShapeDtypeStruct((2, SIDE if before else len(groups), 4, block), jnp.float32)
    return pl.pallas_call(
        functools.partial(score_kernel, groups, each, len(cs), len(before)),
        in_specs=[SCALARS] * 2
        + [OUTSIDE] * (len(groups) + len(cs))
        + [WHOLE] * len(before),
        out_specs=[OUTSIDE, WHOLE],
        scratch_shapes=[
            pltpu.VMEM((2, *xs[0].shape), jnp.bfloat16),
            pltpu.VMEM((2, block, features), jnp.bfloat16),
            pltpu.VMEM((2, 4, block, block), jnp.float32),
            pltpu.SemaphoreType.DMA((2,)),
            pltpu.SemaphoreType.DMA((2,)),
            pltpu.SemaphoreType.DMA((2,)),
        ],
        out_shape=[
            jax.ShapeDtypeStruct((len(pairs), 4, block, block), jnp.float32),
            stat,
        ],
        compiler_params=pltpu.CompilerParams(vmem_limit_bytes=VMEM),
        cost_estimate=spent(2 * len(pairs)),
        name="scores",
    )(tab, seq, *operands)


def sum_kernel(tab, *refs):
    x_refs, refs = refs[:SIDE], refs[SIDE:]
    near, middle, last, *stats = refs[:7]
    far_up, far_down, up, down, here, line = refs[7:13]
    m_ref, r_ref, xbuf, acc, macc, total, stage, sbuf, xsem, sem, stage_sem, score_sem = refs[13:]
    block = acc.shape[0]

    def owner_of(at):
        j = at // SIDE
        return jnp.where(j == 0, 2, jnp.where(j == 1, 1, jnp.where(j == 2, 3, 0)))

    def start_scores(at):
        r, owner = lax.rem(at, SIDE), owner_of(at)
        group = jnp.where(r == 3, 2, r)
        place = jnp.where(owner == 3, 2, owner)
        slot = lax.rem(at, 2)
        far = owner == 2
        for ref, wanted, which in (
            (last, far, jnp.where(r == 2, 3, group)),
            (near, ~far & (r != 2), len(OWNERS) * group + place),
            (middle, ~far & (r == 2), place),
        ):
            for p in range(4):

                @pl.when(wanted & (tab[MASK + 4 * (SIDE * r + owner) + p] == 1))
                def _():
                    pltpu.make_async_copy(
                        ref.at[which, p], sbuf.at[slot, p], score_sem.at[slot]
                    ).start()

    def one_pair(r, owner, at, write):
        slot = r % 2

        @pl.when(at < PAIRS - 1)
        def _():
            start_scores(at + 1)

        for p in range(4):

            @pl.when(tab[MASK + 4 * (SIDE * r + owner) + p] == 1)
            def _():
                pltpu.make_async_copy(
                    last.at[0, p], sbuf.at[slot, p], score_sem.at[slot]
                ).wait()

        mask_at = MASK + 4 * (SIDE * r + owner)
        first = jnp.int32(3)
        for p in (2, 1, 0):
            first = jnp.where(tab[mask_at + p] == 1, p, first)

        def one_block(p, carry):
            def terms():
                shares = (
                    jnp.exp(sbuf[slot, p] - m_ref[r, pl.ds(p, 1), :]) * r_ref[r, pl.ds(p, 1), :]
                )
                product = lax.dot_general(
                    shares.astype(jnp.bfloat16),
                    xbuf[r, pl.ds(pl.multiple_of(p * block, block), block), :],
                    (((1,), (0,)), ((), ())),
                    preferred_element_type=jnp.float32,
                )
                return product, shares[:, :128] + shares[:, 128:]

            @pl.when(p == first)
            def _():
                acc[...], macc[...] = terms()

            @pl.when((p > first) & (tab[mask_at + p] == 1))
            def _():
                product, mass = terms()
                acc[...] += product
                macc[...] += mass

            return carry

        lax.fori_loop(0, 4, one_block, 0)
        mass = jnp.sum(jnp.transpose(macc[...]), axis=0, keepdims=True)

        @pl.when(at >= 2)
        def _():
            stage_copy(here, 0, slot).wait()

        stage[slot, 0:block, :] = acc[:, Z_FIRST:].astype(jnp.bfloat16)
        stage[slot, block:, 0:block] = jnp.broadcast_to(mass, (16, block)).astype(jnp.bfloat16)
        stage[slot, block:, block:] = jnp.zeros((16, stage.shape[2] - block), jnp.bfloat16)
        write(slot)

    def stage_copy(out, at, slot):
        return pltpu.make_async_copy(stage.at[slot], out.at[at], stage_sem.at[slot])

    def add_line(r, owner, slot):
        bid = tab[BID + SIDE * r + owner]
        for i in range(block // 16):
            part = acc[16 * i : 16 * i + 16, :Z_FIRST].astype(jnp.bfloat16)
            total[slot, i, bid] += part.astype(jnp.float32)

    def line_copy(owner, slot):
        return pltpu.make_async_copy(total.at[slot], line.at[:, owner], sem.at[slot])

    def x_copy(r):
        return pltpu.make_async_copy(x_refs[r], xbuf.at[r], xsem.at[r])

    x_copy(0).start()
    start_scores(jnp.int32(0))
    for r in range(SIDE):
        tops = [ref[0, (r - by) % SIDE] for by, ref in enumerate(stats)]
        highest = functools.reduce(jnp.maximum, tops)
        whole = sum(
            ref[1, (r - by) % SIDE] * jnp.exp(tops[by] - highest) for by, ref in enumerate(stats)
        )
        m_ref[r] = highest
        r_ref[r] = 1.0 / whole
    total[0] = jnp.zeros(total.shape[1:], jnp.float32)
    for r in range(SIDE):
        if r + 1 < SIDE:
            x_copy(r + 1).start()
        x_copy(r).wait()
        out = (far_up, far_down)[r // 2]
        one_pair(r, 2, jnp.int32(r), lambda slot: stage_copy(out, r % 2, slot).start())
        add_line(r, 2, 0)
    line_copy(2, 0).start()

    def one_owner(j, carry):
        owner = owner_of(SIDE * (j + 1))
        slot = lax.rem(j + 1, 2)

        @pl.when(j >= 1)
        def _():
            line_copy(owner, slot).wait()

        total[slot] = jnp.zeros(total.shape[1:], jnp.float32)
        for r in range(SIDE):

            def write(slot):
                for i, out in enumerate((up, down, here)):

                    @pl.when(j == i)
                    def _():
                        stage_copy(out, r, slot).start()

            one_pair(r, owner, SIDE * (j + 1) + r, write)
            add_line(r, owner, slot)
        line_copy(owner, slot).start()
        return carry

    lax.fori_loop(0, 3, one_owner, 0)
    for slot in range(2):
        line_copy(0, slot).wait()
        stage_copy(here, 0, slot).wait()


def sum_call(tab, xs, scores, stats, own_blocks):
    block = scores[0].shape[-1]
    features = xs[0].shape[1]
    parts = block // 16
    part = (own_blocks, 16, Z_FIRST)
    return pl.pallas_call(
        sum_kernel,
        in_specs=[SCALARS] + [OUTSIDE] * (SIDE + 3) + [WHOLE] * SIDE,
        out_specs=[OUTSIDE] * 6,
        scratch_shapes=[
            pltpu.VMEM((SIDE, 4, block), jnp.float32),
            pltpu.VMEM((SIDE, 4, block), jnp.float32),
            pltpu.VMEM((SIDE, *xs[0].shape), jnp.bfloat16),
            pltpu.VMEM((block, features), jnp.float32),
            pltpu.VMEM((block, 128), jnp.float32),
            pltpu.VMEM((2, parts, *part), jnp.float32),
            pltpu.VMEM((2, block + 16, features - Z_FIRST), jnp.bfloat16),
            pltpu.VMEM((2, 4, block, block), jnp.float32),
            pltpu.SemaphoreType.DMA((SIDE,)),
            pltpu.SemaphoreType.DMA((2,)),
            pltpu.SemaphoreType.DMA((2,)),
            pltpu.SemaphoreType.DMA((2,)),
        ],
        out_shape=[
            jax.ShapeDtypeStruct((n, block + 16, features - Z_FIRST), jnp.bfloat16)
            for n in (2, 2, 4, 4, 4)
        ]
        + [jax.ShapeDtypeStruct((parts, SIDE, *part), jnp.float32)],
        compiler_params=pltpu.CompilerParams(vmem_limit_bytes=VMEM),
        cost_estimate=spent(0),
        name="sums",
    )(tab, *[xs[r] for r in range(SIDE)], *scores, *stats)


def merge_kernel(ids, *refs):
    arrays, (out, buf, odd, sem) = refs[:-4], refs[-4:]
    entries = [(ref, i) for ref in arrays for i in range(ref.shape[0])]

    def copy(k, slot):
        return pltpu.make_async_copy(buf.at[slot], out.at[k], sem.at[slot])

    def one_part(k, carry):
        slot = lax.rem(k, 2)

        @pl.when(k >= 2)
        def _():
            copy(k, slot).wait()

        first = pl.multiple_of(32 * k + 16 * ids[len(entries)], 16)
        buf[slot] = jnp.zeros(buf.shape[1:], jnp.float32)
        odd[...] = jnp.zeros(odd.shape, jnp.float32)
        for e, (ref, i) in enumerate(entries):
            rows = ref[i, pl.ds(first, 16), :].astype(jnp.float32)
            if e % 2:
                odd[ids[e]] += rows
            else:
                buf[slot, ids[e]] += rows
        buf[slot] += odd[...]
        copy(k, slot).start()
        return carry

    lax.fori_loop(0, out.shape[0], one_part, 0)
    for slot in range(2):
        copy(0, slot).wait()


def merge_call(ids, side, arrays, own_blocks):
    _, tall, features = arrays[0].shape
    part = (own_blocks, 16, features)
    return pl.pallas_call(
        merge_kernel,
        in_specs=[SCALARS] + [WHOLE] * len(arrays),
        out_specs=OUTSIDE,
        scratch_shapes=[
            pltpu.VMEM((2, *part), jnp.float32),
            pltpu.VMEM(part, jnp.float32),
            pltpu.SemaphoreType.DMA((2,)),
        ],
        out_shape=jax.ShapeDtypeStruct((tall // 32, *part), jnp.float32),
        compiler_params=pltpu.CompilerParams(vmem_limit_bytes=VMEM // 3),
        cost_estimate=spent(0),
        name="merge",
    )(jnp.concatenate([ids, side.reshape(1)]), *arrays)


def mass_kernel(ids, *refs):
    arrays, out = refs[:-1], refs[-1]
    entries = [(ref, i) for ref in arrays for i in range(ref.shape[0])]
    out[...] = jnp.zeros(out.shape, jnp.float32)
    for e, (ref, i) in enumerate(entries):
        out[ids[e]] += ref[i][:, : out.shape[-1]].astype(jnp.float32)[0:8]


def mass_call(ids, arrays, own_blocks):
    _, tall, features = arrays[0].shape
    block = tall - 16
    return pl.pallas_call(
        mass_kernel,
        grid_spec=pltpu.PrefetchScalarGridSpec(
            num_scalar_prefetch=1,
            grid=(1,),
            in_specs=[
                pl.BlockSpec((a.shape[0], 16, features), lambda i, ids: (0, block // 16, 0))
                for a in arrays
            ],
            out_specs=pl.BlockSpec((own_blocks, 8, block), lambda i, ids: (0, 0, 0)),
        ),
        out_shape=jax.ShapeDtypeStruct((own_blocks, 8, block), jnp.float32),
        cost_estimate=spent(0),
        name="masses",
    )(ids, *arrays)


def pick_kernel(tab, low, high, beside, *refs):
    picked, part, same, xbuf, cbuf, xsem, csem = refs[-7:]
    share = part.shape[0]
    core = tab[CORE]
    pltpu.make_async_copy(beside.at[pl.ds(core * share, share)], cbuf, csem).start()
    for side, ref in enumerate((low, high)):

        @pl.when(core == side)
        def _():
            pltpu.make_async_copy(ref, xbuf, xsem).start()

    outward = ((xbuf, picked, xsem), (cbuf, part, csem))
    for buf, out, sem in outward:
        pltpu.make_async_copy(buf, buf, sem).wait()
        pltpu.make_async_copy(buf, out, sem).start()
    for buf, out, sem in outward:
        pltpu.make_async_copy(buf, out, sem).wait()


def pick_call(tab, low, high, beside):
    half = (beside.shape[0] // 2, *beside.shape[1:])
    return pl.pallas_call(
        pick_kernel,
        in_specs=[SCALARS] + [OUTSIDE] * 3,
        out_specs=[OUTSIDE] * 3,
        scratch_shapes=[
            pltpu.VMEM(low.shape, low.dtype),
            pltpu.VMEM(half, beside.dtype),
            pltpu.SemaphoreType.DMA,
            pltpu.SemaphoreType.DMA,
        ],
        out_shape=[
            jax.ShapeDtypeStruct(low.shape, low.dtype),
            jax.ShapeDtypeStruct(half, beside.dtype),
            jax.ShapeDtypeStruct(beside.shape, beside.dtype),
        ],
        input_output_aliases={3: 2},
        compiler_params=pltpu.CompilerParams(vmem_limit_bytes=VMEM),
        cost_estimate=spent(0),
        name="pick",
    )(tab, low, high, beside)


def shift_x(value, by):
    pairs = [
        (SIDE * x + y, SIDE * ((x + by) % SIDE) + y) for x in range(SIDE) for y in range(SIDE)
    ]
    return lax.ppermute(value, "cent", pairs)


def shift_y(value, by):
    pairs = [
        (SIDE * x + y, SIDE * x + (y + by) % SIDE) for x in range(SIDE) for y in range(SIDE)
    ]
    return lax.ppermute(value, "cent", pairs)


def from_either(value):
    n = PAIRS
    pairs = []
    for dp in range(16):
        for x in range(SIDE):
            for y in range(SIDE):
                source = (x + (-1 if dp % 2 == 0 else 1)) % SIDE
                pairs.append((dp * n + SIDE * source + y, dp * n + SIDE * x + y))
    return lax.ppermute(value, ("dp", "cent"), pairs)


def from_beside(value):
    n = PAIRS
    pairs = []
    for dp in range(16):
        for x in range(SIDE):
            for y in range(SIDE):
                source = (y + (1 if dp % 2 == 0 else -1)) % SIDE
                pairs.append((dp * n + SIDE * x + source, dp * n + SIDE * x + y))
    return lax.ppermute(value, ("dp", "cent"), pairs)


def swap_core(value):
    return lax.ppermute(value, "dp", [(i, i ^ 1) for i in range(16)])


def nothing(*arrays):
    return sum(jnp.minimum(jnp.abs(a[0, 0]), 0) for a in arrays)


def tables(candidates, own_blocks):
    place = lax.axis_index("cent")
    x, y = place // SIDE, place % SIDE
    core = (lax.axis_index("dp") % 2).astype(jnp.int32)
    n, each = candidates.shape
    padded = jnp.pad(candidates, ((0, PAD_ROWS - n), (0, 256 - each)))
    every = lax.all_gather(padded, "cent", axis=0, tiled=True)
    every = every.reshape(SIDE, SIDE, PAD_ROWS, 256)[:, :, :n, :each]
    near = jnp.roll(every, (-x, -y), axis=(0, 1))
    owner, local = near // own_blocks, near % own_blocks
    line = SIDE * x + (y + jnp.arange(SIDE, dtype=jnp.int32)) % SIDE
    named = owner[:, 0][:, None] == line[None, :, None, None]
    bid = jnp.max(jnp.where(named, local[:, 0][:, None], 0), axis=(2, 3)).astype(jnp.int32)
    mask = jnp.any(named, axis=3).astype(jnp.int32)
    tab = jnp.concatenate([bid.reshape(-1), mask.reshape(-1), core.reshape(1)])
    mine = jnp.max(jnp.where(owner == place, local, 0), axis=(2, 3)).astype(jnp.int32)
    return tab, mine, core


def per_device(points, candidates, centroids):
    own_blocks, block, features = centroids.shape
    stripe = lax.axis_size("dp")
    rows_each = block // stripe
    dp_place = lax.axis_index("dp")
    tab, mine, core = tables(candidates, own_blocks)

    x3, x1 = shift_x(points, 1), shift_x(points, -1)
    handed, part, beside = pick_call(tab, x3, x1, from_beside(centroids))
    x2 = from_either(handed)
    opposite = from_beside(part)
    xs = {0: points, 1: x1, 2: x2, 3: x3}
    cs = [centroids, beside, swap_core(beside)]
    near, near_stats = score_call(tab, NEAR, xs, cs)
    opposite += nothing(near_stats[0, 0]).astype(opposite.dtype)
    middle, middle_stats = score_call(tab, MIDDLE, xs, cs)
    cs += [opposite, swap_core(opposite)]
    last, stats = score_call(tab, LAST, xs, cs, (near_stats, middle_stats))

    stats = [stats] + [shift_x(stats, -by) for by in (1, 2, 3)]
    lines = [[2 * z + c for z in range(stripe // 2)] for c in range(2)]

    def over_z(sums, other):
        both = sums + swap_core(other)
        return lax.psum_scatter(
            both, "dp", scatter_dimension=0, axis_index_groups=lines, tiled=True
        )[0]

    far_up, far_down, up, down, here, line = sum_call(
        tab, xs, (near, middle, last), stats, own_blocks
    )
    line = lax.psum_scatter(line, "dp", scatter_dimension=0, tiled=True)[0]
    far_up, far_down = shift_y(far_up, 1), shift_y(far_down, -1)
    up, down = shift_y(up, 1), shift_y(down, -1)
    far_up, far_down = shift_y(far_up, 1), shift_y(far_down, -1)
    ids = jnp.concatenate([mine[:, 0], mine[:, 2], mine[:, 3], mine[:, 1]])
    arrays = (here, far_up, far_down, up, down)
    other = merge_call(ids, 1 - core, arrays, own_blocks)
    sums = over_z(merge_call(ids, core, arrays, own_blocks), other)
    line = line[0] + shift_y(line[1], 1) + shift_y(line[2], 2) + shift_y(line[3], -1)
    mass = mass_call(ids, arrays, own_blocks)[:, 0, :]
    mass = mass.reshape(own_blocks, stripe, rows_each).transpose(1, 0, 2)
    mass = lax.all_to_all(mass, "dp", split_axis=0, concat_axis=0, tiled=True)
    new_mass = jnp.sum(mass, axis=0)
    previous = lax.dynamic_slice_in_dim(centroids, dp_place * rows_each, rows_each, 1).astype(
        jnp.float32
    )
    new_sums = jnp.concatenate([line, sums], axis=2)
    return (new_sums + previous) / (new_mass + 1.0)[:, :, None], new_mass


def solution(mesh):
    in_specs = (P(("dp", "cent"), None), P(("dp", "cent"), None), P("cent", None, None))
    out_specs = (P("cent", "dp", None), P("cent", "dp"))
    return jax.shard_map(
        per_device, mesh=mesh, in_specs=in_specs, out_specs=out_specs, check_vma=False
    )
```

```python
import functools

import jax
import jax.numpy as jnp
from jax import lax
from jax.experimental import pallas as pl
from jax.experimental.pallas import tpu as pltpu
from jax.sharding import PartitionSpec as P

SIDE = 4
PAIRS = SIDE * SIDE
inverse_temp = 0.03125
LOW = -1e30
VMEM = 56 * 1024 * 1024
PAD_ROWS = 64
Z_FIRST = 384
BID, MASK, CORE = 0, PAIRS, PAIRS + 4 * PAIRS
GROUPS, OWNERS = (0, 1, 3), (0, 1, 3)
NEAR = [(r, s) for r in GROUPS for s in OWNERS]
MIDDLE = [(2, s) for s in OWNERS]
LAST = [(r, 2) for r in (0, 1, 3, 2)]
WHOLE = pl.BlockSpec(memory_space=pltpu.VMEM)
SCALARS = pl.BlockSpec(memory_space=pltpu.SMEM)
OUTSIDE = pl.BlockSpec(memory_space=pltpu.HBM)


def spent(us):
    return pl.CostEstimate(flops=1000, bytes_accessed=1000 + 3_000_000 * us, transcendentals=0)


def score_kernel(groups, each, n_c, n_before, tab, seq, *refs):
    x_refs, refs = refs[: len(groups)], refs[len(groups) :]
    c_refs, refs = refs[:n_c], refs[n_c:]
    before, refs = refs[:n_before], refs[n_before:]
    score_ref, stat_ref, xbuf, cbuf, sbuf, xsem, csem, ssem = refs
    block = cbuf.shape[1]
    total = each * len(groups)

    def score_copy(at, p):
        slot = lax.rem(at, 2)
        return pltpu.make_async_copy(sbuf.at[slot, p], score_ref.at[at, p], ssem.at[slot])

    def wait_scores(at):
        pair = SIDE * seq[2 * at] + seq[2 * at + 1]
        for p in range(4):

            @pl.when(tab[MASK + 4 * pair + p] == 1)
            def _():
                score_copy(at, p).wait()

    def start_c(at):
        r, owner = seq[2 * at], seq[2 * at + 1]
        slot = lax.rem(at, 2)
        bid = tab[BID + SIDE * r + owner]
        core = tab[CORE]
        side = jnp.where(owner == 2, bid // 4, jnp.where(owner == 1, 0, 1))
        beside = (owner == 1) | (owner == 3)
        wanted = (
            owner == 0,
            beside & (side == core),
            beside & (side != core),
            (owner == 2) & (side == core),
            (owner == 2) & (side != core),
        )
        for ref, here in zip(c_refs, wanted):

            @pl.when(here)
            def _():
                pltpu.make_async_copy(
                    ref.at[lax.rem(bid, ref.shape[0])], cbuf.at[slot], csem.at[slot]
                ).start()

    def x_copy(g):
        return pltpu.make_async_copy(x_refs[g], xbuf.at[g % 2], xsem.at[g % 2])

    x_copy(0).start()
    start_c(jnp.int32(0))
    for g, r in enumerate(groups):
        if g + 1 < len(groups):
            x_copy(g + 1).start()
        x_copy(g).wait()
        if n_before:
            source = 0 if r in GROUPS else 1
            place = GROUPS.index(r) if r in GROUPS else 0
            at = r
            stat_ref[0, at] = before[source][0, place]
            stat_ref[1, at] = before[source][1, place]
        else:
            at = g
            stat_ref[0, at] = jnp.full(stat_ref.shape[2:], LOW, jnp.float32)
            stat_ref[1, at] = jnp.zeros(stat_ref.shape[2:], jnp.float32)

        def one_owner(j, carry, g=g, r=r, at=at):
            step = each * g + j
            cslot = lax.rem(step, 2)

            @pl.when(step < total - 1)
            def _():
                start_c(step + 1)

            @pl.when(step >= 2)
            def _():
                wait_scores(step - 2)

            pltpu.make_async_copy(cbuf.at[cslot], cbuf.at[cslot], csem.at[cslot]).wait()
            wide = cbuf[cslot].astype(jnp.float32)
            half_norm = 0.5 * jnp.sum(wide * wide, axis=1, keepdims=True)
            mask_at = MASK + 4 * (SIDE * r + seq[2 * step + 1])

            def one_block(p, carry):
                @pl.when(tab[mask_at + p] == 1)
                def _():
                    x = xbuf[g % 2, pl.ds(pl.multiple_of(p * block, block), block), :]
                    dots = lax.dot_general(
                        cbuf[cslot], x, (((1,), (1,)), ((), ())), preferred_element_type=jnp.float32
                    )
                    scores = (dots - half_norm) * inverse_temp
                    sbuf[cslot, p] = scores
                    score_copy(step, p).start()
                    old = stat_ref[0, at, pl.ds(p, 1), :]
                    new = jnp.maximum(old, jnp.max(scores, axis=0, keepdims=True))
                    stat_ref[0, at, pl.ds(p, 1), :] = new
                    stat_ref[1, at, pl.ds(p, 1), :] = stat_ref[1, at, pl.ds(p, 1), :] * jnp.exp(
                        old - new
                    ) + jnp.sum(jnp.exp(scores - new), axis=0, keepdims=True)

                return carry

            return lax.fori_loop(0, 4, one_block, carry)

        lax.fori_loop(0, each, one_owner, 0)
    for at in (total - 2, total - 1):
        wait_scores(at)


def score_call(tab, pairs, xs, cs, before=()):
    _, block, features = cs[0].shape
    groups = tuple(dict.fromkeys(r for r, _ in pairs))
    each = len(pairs) // len(groups)
    seq = jnp.array([v for pair in pairs for v in pair], jnp.int32)
    operands = [xs[r] for r in groups] + list(cs) + list(before)
    stat = jax.ShapeDtypeStruct((2, SIDE if before else len(groups), 4, block), jnp.float32)
    return pl.pallas_call(
        functools.partial(score_kernel, groups, each, len(cs), len(before)),
        in_specs=[SCALARS] * 2
        + [OUTSIDE] * (len(groups) + len(cs))
        + [WHOLE] * len(before),
        out_specs=[OUTSIDE, WHOLE],
        scratch_shapes=[
            pltpu.VMEM((2, *xs[0].shape), jnp.bfloat16),
            pltpu.VMEM((2, block, features), jnp.bfloat16),
            pltpu.VMEM((2, 4, block, block), jnp.float32),
            pltpu.SemaphoreType.DMA((2,)),
            pltpu.SemaphoreType.DMA((2,)),
            pltpu.SemaphoreType.DMA((2,)),
        ],
        out_shape=[
            jax.ShapeDtypeStruct((len(pairs), 4, block, block), jnp.float32),
            stat,
        ],
        compiler_params=pltpu.CompilerParams(vmem_limit_bytes=VMEM),
        cost_estimate=spent(2 * len(pairs)),
        name="scores",
    )(tab, seq, *operands)


def sum_kernel(tab, *refs):
    x_refs, refs = refs[:SIDE], refs[SIDE:]
    near, middle, last, *stats = refs[:7]
    far_up, far_down, up, down, here, line = refs[7:13]
    m_ref, r_ref, xbuf, acc, macc, total, stage, sbuf, xsem, sem, stage_sem, score_sem = refs[13:]
    block = acc.shape[0]

    def owner_of(at):
        j = at // SIDE
        return jnp.where(j == 0, 2, jnp.where(j == 1, 1, jnp.where(j == 2, 3, 0)))

    def start_scores(at):
        r, owner = lax.rem(at, SIDE), owner_of(at)
        group = jnp.where(r == 3, 2, r)
        place = jnp.where(owner == 3, 2, owner)
        slot = lax.rem(at, 2)
        far = owner == 2
        for ref, wanted, which in (
            (last, far, jnp.where(r == 2, 3, group)),
            (near, ~far & (r != 2), len(OWNERS) * group + place),
            (middle, ~far & (r == 2), place),
        ):
            for p in range(4):

                @pl.when(wanted & (tab[MASK + 4 * (SIDE * r + owner) + p] == 1))
                def _():
                    pltpu.make_async_copy(
                        ref.at[which, p], sbuf.at[slot, p], score_sem.at[slot]
                    ).start()

    def one_pair(r, owner, at, write):
        slot = r % 2

        @pl.when(at < PAIRS - 1)
        def _():
            start_scores(at + 1)

        for p in range(4):

            @pl.when(tab[MASK + 4 * (SIDE * r + owner) + p] == 1)
            def _():
                pltpu.make_async_copy(
                    last.at[0, p], sbuf.at[slot, p], score_sem.at[slot]
                ).wait()

        mask_at = MASK + 4 * (SIDE * r + owner)
        first = jnp.int32(3)
        for p in (2, 1, 0):
            first = jnp.where(tab[mask_at + p] == 1, p, first)

        def one_block(p, carry):
            def terms():
                shares = (
                    jnp.exp(sbuf[slot, p] - m_ref[r, pl.ds(p, 1), :]) * r_ref[r, pl.ds(p, 1), :]
                )
                product = lax.dot_general(
                    shares.astype(jnp.bfloat16),
                    xbuf[r, pl.ds(pl.multiple_of(p * block, block), block), :],
                    (((1,), (0,)), ((), ())),
                    preferred_element_type=jnp.float32,
                )
                return product, shares[:, :128] + shares[:, 128:]

            @pl.when(p == first)
            def _():
                acc[...], macc[...] = terms()

            @pl.when((p > first) & (tab[mask_at + p] == 1))
            def _():
                product, mass = terms()
                acc[...] += product
                macc[...] += mass

            return carry

        lax.fori_loop(0, 4, one_block, 0)
        mass = jnp.sum(jnp.transpose(macc[...]), axis=0, keepdims=True)

        @pl.when(at >= 2)
        def _():
            stage_copy(here, 0, slot).wait()

        stage[slot, 0:block, :] = acc[:, Z_FIRST:].astype(jnp.bfloat16)
        stage[slot, block:, 0:block] = jnp.broadcast_to(mass, (16, block)).astype(jnp.bfloat16)
        stage[slot, block:, block:] = jnp.zeros((16, stage.shape[2] - block), jnp.bfloat16)
        write(slot)

    def stage_copy(out, at, slot):
        return pltpu.make_async_copy(stage.at[slot], out.at[at], stage_sem.at[slot])

    def add_line(r, owner, slot):
        bid = tab[BID + SIDE * r + owner]
        for i in range(block // 16):
            part = acc[16 * i : 16 * i + 16, :Z_FIRST].astype(jnp.bfloat16)
            total[slot, i, bid] += part.astype(jnp.float32)

    def line_copy(owner, slot):
        return pltpu.make_async_copy(total.at[slot], line.at[:, owner], sem.at[slot])

    def x_copy(r):
        return pltpu.make_async_copy(x_refs[r], xbuf.at[r], xsem.at[r])

    x_copy(0).start()
    start_scores(jnp.int32(0))
    for r in range(SIDE):
        tops = [ref[0, (r - by) % SIDE] for by, ref in enumerate(stats)]
        highest = functools.reduce(jnp.maximum, tops)
        whole = sum(
            ref[1, (r - by) % SIDE] * jnp.exp(tops[by] - highest) for by, ref in enumerate(stats)
        )
        m_ref[r] = highest
        r_ref[r] = 1.0 / whole
    total[0] = jnp.zeros(total.shape[1:], jnp.float32)
    for r in range(SIDE):
        if r + 1 < SIDE:
            x_copy(r + 1).start()
        x_copy(r).wait()
        out = (far_up, far_down)[r // 2]
        one_pair(r, 2, jnp.int32(r), lambda slot: stage_copy(out, r % 2, slot).start())
        add_line(r, 2, 0)
    line_copy(2, 0).start()

    def one_owner(j, carry):
        owner = owner_of(SIDE * (j + 1))
        slot = lax.rem(j + 1, 2)

        @pl.when(j >= 1)
        def _():
            line_copy(owner, slot).wait()

        total[slot] = jnp.zeros(total.shape[1:], jnp.float32)
        for r in range(SIDE):

            def write(slot):
                for i, out in enumerate((up, down, here)):

                    @pl.when(j == i)
                    def _():
                        stage_copy(out, r, slot).start()

            one_pair(r, owner, SIDE * (j + 1) + r, write)
            add_line(r, owner, slot)
        line_copy(owner, slot).start()
        return carry

    lax.fori_loop(0, 3, one_owner, 0)
    for slot in range(2):
        line_copy(0, slot).wait()
        stage_copy(here, 0, slot).wait()


def sum_call(tab, xs, scores, stats, own_blocks):
    block = scores[0].shape[-1]
    features = xs[0].shape[1]
    parts = block // 16
    part = (own_blocks, 16, Z_FIRST)
    return pl.pallas_call(
        sum_kernel,
        in_specs=[SCALARS] + [OUTSIDE] * (SIDE + 3) + [WHOLE] * SIDE,
        out_specs=[OUTSIDE] * 6,
        scratch_shapes=[
            pltpu.VMEM((SIDE, 4, block), jnp.float32),
            pltpu.VMEM((SIDE, 4, block), jnp.float32),
            pltpu.VMEM((SIDE, *xs[0].shape), jnp.bfloat16),
            pltpu.VMEM((block, features), jnp.float32),
            pltpu.VMEM((block, 128), jnp.float32),
            pltpu.VMEM((2, parts, *part), jnp.float32),
            pltpu.VMEM((2, block + 16, features - Z_FIRST), jnp.bfloat16),
            pltpu.VMEM((2, 4, block, block), jnp.float32),
            pltpu.SemaphoreType.DMA((SIDE,)),
            pltpu.SemaphoreType.DMA((2,)),
            pltpu.SemaphoreType.DMA((2,)),
            pltpu.SemaphoreType.DMA((2,)),
        ],
        out_shape=[
            jax.ShapeDtypeStruct((n, block + 16, features - Z_FIRST), jnp.bfloat16)
            for n in (2, 2, 4, 4, 4)
        ]
        + [jax.ShapeDtypeStruct((parts, SIDE, *part), jnp.float32)],
        compiler_params=pltpu.CompilerParams(vmem_limit_bytes=VMEM),
        cost_estimate=spent(0),
        name="sums",
    )(tab, *[xs[r] for r in range(SIDE)], *scores, *stats)


def merge_kernel(ids, *refs):
    arrays, (out, buf, odd, sem) = refs[:-4], refs[-4:]
    entries = [(ref, i) for ref in arrays for i in range(ref.shape[0])]

    def copy(k, slot):
        return pltpu.make_async_copy(buf.at[slot], out.at[k], sem.at[slot])

    def one_part(k, carry):
        slot = lax.rem(k, 2)

        @pl.when(k >= 2)
        def _():
            copy(k, slot).wait()

        first = pl.multiple_of(32 * k + 16 * ids[len(entries)], 16)
        buf[slot] = jnp.zeros(buf.shape[1:], jnp.float32)
        odd[...] = jnp.zeros(odd.shape, jnp.float32)
        for e, (ref, i) in enumerate(entries):
            rows = ref[i, pl.ds(first, 16), :].astype(jnp.float32)
            if e % 2:
                odd[ids[e]] += rows
            else:
                buf[slot, ids[e]] += rows
        buf[slot] += odd[...]
        copy(k, slot).start()
        return carry

    lax.fori_loop(0, out.shape[0], one_part, 0)
    for slot in range(2):
        copy(0, slot).wait()


def merge_call(ids, side, arrays, own_blocks):
    _, tall, features = arrays[0].shape
    part = (own_blocks, 16, features)
    return pl.pallas_call(
        merge_kernel,
        in_specs=[SCALARS] + [WHOLE] * len(arrays),
        out_specs=OUTSIDE,
        scratch_shapes=[
            pltpu.VMEM((2, *part), jnp.float32),
            pltpu.VMEM(part, jnp.float32),
            pltpu.SemaphoreType.DMA((2,)),
        ],
        out_shape=jax.ShapeDtypeStruct((tall // 32, *part), jnp.float32),
        compiler_params=pltpu.CompilerParams(vmem_limit_bytes=VMEM // 3),
        cost_estimate=spent(0),
        name="merge",
    )(jnp.concatenate([ids, side.reshape(1)]), *arrays)


def mass_kernel(ids, *refs):
    arrays, out = refs[:-1], refs[-1]
    entries = [(ref, i) for ref in arrays for i in range(ref.shape[0])]
    out[...] = jnp.zeros(out.shape, jnp.float32)
    for e, (ref, i) in enumerate(entries):
        out[ids[e]] += ref[i][:, : out.shape[-1]].astype(jnp.float32)[0:8]


def mass_call(ids, arrays, own_blocks):
    _, tall, features = arrays[0].shape
    block = tall - 16
    return pl.pallas_call(
        mass_kernel,
        grid_spec=pltpu.PrefetchScalarGridSpec(
            num_scalar_prefetch=1,
            grid=(1,),
            in_specs=[
                pl.BlockSpec((a.shape[0], 16, features), lambda i, ids: (0, block // 16, 0))
                for a in arrays
            ],
            out_specs=pl.BlockSpec((own_blocks, 8, block), lambda i, ids: (0, 0, 0)),
        ),
        out_shape=jax.ShapeDtypeStruct((own_blocks, 8, block), jnp.float32),
        cost_estimate=spent(0),
        name="masses",
    )(ids, *arrays)


def pick_kernel(tab, low, high, beside, *refs):
    picked, part, same, xbuf, cbuf, xsem, csem = refs[-7:]
    share = part.shape[0]
    core = tab[CORE]
    pieces = xsem.shape[0]
    rows, blocks = xbuf.shape[0] // pieces, share // pieces
    for i in range(pieces):
        for side, ref in enumerate((low, high)):

            @pl.when(core == side)
            def _():
                here = pl.ds(i * rows, rows)
                pltpu.make_async_copy(ref.at[here], xbuf.at[here], xsem.at[i]).start()

        pltpu.make_async_copy(
            beside.at[pl.ds(core * share + i * blocks, blocks)],
            cbuf.at[pl.ds(i * blocks, blocks)],
            csem.at[i],
        ).start()

    def outward(i):
        return [
            pltpu.make_async_copy(buf.at[pl.ds(i * n, n)], out.at[pl.ds(i * n, n)], sem.at[i])
            for buf, out, sem, n in ((xbuf, picked, xsem, rows), (cbuf, part, csem, blocks))
        ]

    for i in range(pieces):
        for copy in outward(i):
            copy.wait()
            copy.start()
    for i in range(pieces):
        for copy in outward(i):
            copy.wait()


def pick_call(tab, low, high, beside):
    half = (beside.shape[0] // 2, *beside.shape[1:])
    return pl.pallas_call(
        pick_kernel,
        in_specs=[SCALARS] + [OUTSIDE] * 3,
        out_specs=[OUTSIDE] * 3,
        scratch_shapes=[
            pltpu.VMEM(low.shape, low.dtype),
            pltpu.VMEM(half, beside.dtype),
            pltpu.SemaphoreType.DMA((4,)),
            pltpu.SemaphoreType.DMA((4,)),
        ],
        out_shape=[
            jax.ShapeDtypeStruct(low.shape, low.dtype),
            jax.ShapeDtypeStruct(half, beside.dtype),
            jax.ShapeDtypeStruct(beside.shape, beside.dtype),
        ],
        input_output_aliases={3: 2},
        compiler_params=pltpu.CompilerParams(vmem_limit_bytes=VMEM),
        cost_estimate=spent(0),
        name="pick",
    )(tab, low, high, beside)


def after_call(value, other):
    return pl.pallas_call(
        lambda value, other, out: None,
        in_specs=[OUTSIDE] * 2,
        out_specs=OUTSIDE,
        out_shape=jax.ShapeDtypeStruct(value.shape, value.dtype),
        input_output_aliases={0: 0},
        cost_estimate=spent(0),
        name="after",
    )(value, other)


def shift_x(value, by):
    pairs = [
        (SIDE * x + y, SIDE * ((x + by) % SIDE) + y) for x in range(SIDE) for y in range(SIDE)
    ]
    return lax.ppermute(value, "cent", pairs)


def shift_y(value, by):
    pairs = [
        (SIDE * x + y, SIDE * x + (y + by) % SIDE) for x in range(SIDE) for y in range(SIDE)
    ]
    return lax.ppermute(value, "cent", pairs)


def from_either(value):
    n = PAIRS
    pairs = []
    for dp in range(16):
        for x in range(SIDE):
            for y in range(SIDE):
                source = (x + (-1 if dp % 2 == 0 else 1)) % SIDE
                pairs.append((dp * n + SIDE * source + y, dp * n + SIDE * x + y))
    return lax.ppermute(value, ("dp", "cent"), pairs)


def from_beside(value):
    n = PAIRS
    pairs = []
    for dp in range(16):
        for x in range(SIDE):
            for y in range(SIDE):
                source = (y + (1 if dp % 2 == 0 else -1)) % SIDE
                pairs.append((dp * n + SIDE * x + source, dp * n + SIDE * x + y))
    return lax.ppermute(value, ("dp", "cent"), pairs)


def swap_core(value):
    return lax.ppermute(value, "dp", [(i, i ^ 1) for i in range(16)])


def tables(candidates, own_blocks):
    place = lax.axis_index("cent")
    x, y = place // SIDE, place % SIDE
    core = (lax.axis_index("dp") % 2).astype(jnp.int32)
    n, each = candidates.shape
    padded = jnp.pad(candidates, ((0, PAD_ROWS - n), (0, 256 - each)))
    every = lax.all_gather(padded, "cent", axis=0, tiled=True)
    every = every.reshape(SIDE, SIDE, PAD_ROWS, 256)[:, :, :n, :each]
    near = jnp.roll(every, (-x, -y), axis=(0, 1))
    owner, local = near // own_blocks, near % own_blocks
    line = SIDE * x + (y + jnp.arange(SIDE, dtype=jnp.int32)) % SIDE
    named = owner[:, 0][:, None] == line[None, :, None, None]
    bid = jnp.max(jnp.where(named, local[:, 0][:, None], 0), axis=(2, 3)).astype(jnp.int32)
    mask = jnp.any(named, axis=3).astype(jnp.int32)
    tab = jnp.concatenate([bid.reshape(-1), mask.reshape(-1), core.reshape(1)])
    mine = jnp.max(jnp.where(owner == place, local, 0), axis=(2, 3)).astype(jnp.int32)
    return tab, mine, core


def per_device(points, candidates, centroids):
    own_blocks, block, features = centroids.shape
    stripe = lax.axis_size("dp")
    rows_each = block // stripe
    dp_place = lax.axis_index("dp")
    tab, mine, core = tables(candidates, own_blocks)

    x3, x1 = shift_x(points, 1), shift_x(points, -1)
    handed, part, beside = pick_call(tab, x3, x1, from_beside(centroids))
    x2 = from_either(handed)
    opposite = from_beside(part)
    xs = {0: points, 1: x1, 2: x2, 3: x3}
    cs = [centroids, beside, swap_core(beside)]
    near, near_stats = score_call(tab, NEAR, xs, cs)
    opposite = after_call(opposite, near_stats)
    middle, middle_stats = score_call(tab, MIDDLE, xs, cs)
    cs += [opposite, swap_core(opposite)]
    last, stats = score_call(tab, LAST, xs, cs, (near_stats, middle_stats))

    stats = [stats] + [shift_x(stats, -by) for by in (1, 2, 3)]
    lines = [[2 * z + c for z in range(stripe // 2)] for c in range(2)]

    def over_z(sums, other):
        both = sums + swap_core(other)
        return lax.psum_scatter(
            both, "dp", scatter_dimension=0, axis_index_groups=lines, tiled=True
        )[0]

    far_up, far_down, up, down, here, line = sum_call(
        tab, xs, (near, middle, last), stats, own_blocks
    )
    line = lax.psum_scatter(line, "dp", scatter_dimension=0, tiled=True)[0]
    far_up, far_down = shift_y(far_up, 1), shift_y(far_down, -1)
    up, down = shift_y(up, 1), shift_y(down, -1)
    far_up, far_down = shift_y(far_up, 1), shift_y(far_down, -1)
    ids = jnp.concatenate([mine[:, 0], mine[:, 2], mine[:, 3], mine[:, 1]])
    arrays = (here, far_up, far_down, up, down)
    other = merge_call(ids, 1 - core, arrays, own_blocks)
    sums = over_z(merge_call(ids, core, arrays, own_blocks), other)
    line = line[0] + shift_y(line[1], 1) + shift_y(line[2], 2) + shift_y(line[3], -1)
    mass = mass_call(ids, arrays, own_blocks)[:, 0, :]
    mass = mass.reshape(own_blocks, stripe, rows_each).transpose(1, 0, 2)
    mass = lax.all_to_all(mass, "dp", split_axis=0, concat_axis=0, tiled=True)
    new_mass = jnp.sum(mass, axis=0)
    previous = lax.dynamic_slice_in_dim(centroids, dp_place * rows_each, rows_each, 1).astype(
        jnp.float32
    )
    new_sums = jnp.concatenate([line, sums], axis=2)
    return (new_sums + previous) / (new_mass + 1.0)[:, :, None], new_mass


def solution(mesh):
    in_specs = (P(("dp", "cent"), None), P(("dp", "cent"), None), P("cent", None, None))
    out_specs = (P("cent", "dp", None), P("cent", "dp"))
    return jax.shard_map(
        per_device, mesh=mesh, in_specs=in_specs, out_specs=out_specs, check_vma=False
    )
```
